512 devices in a mesh: rows: 128 (over z, y, core), rep: 4 (over x).
Axes of the slice: x: 4, y: 8, z: 8, core: 2. Of those that a mesh axis runs over, the one named last changes fastest.
Arguments:
- features: bfloat16 [32768, 256], P('rows'), may hold values from -6 to 6
- weight: bfloat16 [256, 256], replicated, may hold values from -0.375 to 0.375
- cotangent: bfloat16 [32768, 256], P('rows'), may hold values from -6 to 6
- tile_coords: int32 [128, 4, 20, 2], P('rows', 'rep'), may hold values from 0 to 255, as said below
- tile_count: int32 [128, 4], P('rows', 'rep'), may hold values from 0 to 20, as said below
- tiles: bfloat16 [128, 4, 20, 128, 128], P('rows', 'rep'), as said below
Outputs:
- activation: bfloat16 [32768, 256], P('rows')
- input_grad: bfloat16 [32768, 256], P('rows')
- weight_grad: float32 [256, 256], replicated
The draws below stay inside these ranges and needn't reach their ends.
Inputs may be any that keep to these rules, and one draw needn't show every extreme that they name: `tile_coords`: entry k of device (i, j)'s list holds a tile row below 2 and a global tile column c with (c // 2) % 4 == j; live entries come first and name distinct tiles; every nonzero tile of A is listed on exactly one device; padding entries hold tile row 0 and a column of the device's first section. `tile_count`: in every draw some device's list is full. `tiles`: A is symmetric: the tile at (r, c) is the transpose of the tile at (c, r); slots at or beyond a device's tile_count hold zeros.
All inputs are finite; a program needn't handle non-finite values.
Results may differ from the reference program's by a relative error of at most 0.006.
Values may be sent and summed in bfloat16 or wider, within the bound.
A program may use at most 64 MiB of HBM per device.

```python
import math
import jax
import jax.numpy as jnp
from jax import lax

F = 256
TILE = 128
ROWS_DEV = 256
NOFF = 4
KMAX = 20
NODES = 32768
N_ROWS = 128
N_REP = 4


def tile_layout(key):
    per_dev = ROWS_DEV // TILE
    tile_total = NODES // TILE
    section_total = N_ROWS // N_REP
    key_offsets, key_central, key_hub = jax.random.split(key, 3)
    others = jax.random.permutation(key_offsets, tile_total // 2 - 1)[:NOFF - 1] + 1
    offsets = jnp.concatenate([jnp.full((1,), tile_total // 2, others.dtype), others])
    central = jax.random.randint(key_central, (), 0, N_ROWS)
    tile_ids = jnp.arange(tile_total)
    block_of = tile_ids // per_dev
    spacing = (tile_ids[None, :] - tile_ids[:, None]) % tile_total
    near = jnp.any((spacing[:, :, None] == offsets[None, None, :]) | (spacing[:, :, None] == tile_total - offsets[None, None, :]), axis=-1)
    outside = block_of != central
    drawn = near & outside[:, None] & outside[None, :]
    cand_shape = (N_REP, per_dev, section_total, per_dev)
    cand_total = per_dev * section_total * per_dev
    rep_axis = jnp.arange(N_REP).reshape(N_REP, 1, 1, 1)
    row_axis = jnp.arange(per_dev).reshape(1, per_dev, 1, 1)
    section_axis = jnp.arange(section_total).reshape(1, 1, section_total, 1)
    col_axis = jnp.arange(per_dev).reshape(1, 1, 1, per_dev)
    cand_block = jnp.broadcast_to(section_axis * N_REP + rep_axis, cand_shape).reshape(N_REP, cand_total)
    cand_row = jnp.broadcast_to(central * per_dev + row_axis, cand_shape).reshape(N_REP, cand_total)
    cand_col = jnp.broadcast_to((section_axis * N_REP + rep_axis) * per_dev + col_axis, cand_shape).reshape(N_REP, cand_total)
    eligible = cand_block != central
    shuffled = jax.random.permutation(key_hub, N_REP * cand_total).reshape(N_REP, cand_total)
    score = jnp.where(eligible, shuffled, shuffled + N_REP * cand_total)
    order = jnp.argsort(score, axis=-1)
    placing = jnp.argsort(order, axis=-1)
    chosen = ((placing < KMAX) & eligible).astype(jnp.int32)
    hub = jnp.zeros((tile_total, tile_total), jnp.int32).at[cand_row.reshape(-1), cand_col.reshape(-1)].add(chosen.reshape(-1))
    present = drawn | (hub > 0) | (hub.T > 0)
    shape = (N_ROWS, N_REP, per_dev, section_total, per_dev)
    device_row = jnp.arange(N_ROWS).reshape(N_ROWS, 1, 1, 1, 1)
    rep_index = jnp.arange(N_REP).reshape(1, N_REP, 1, 1, 1)
    local_row = jnp.arange(per_dev).reshape(1, 1, per_dev, 1, 1)
    section_step = jnp.arange(section_total).reshape(1, 1, 1, section_total, 1)
    local_col = jnp.arange(per_dev).reshape(1, 1, 1, 1, per_dev)
    global_row = jnp.broadcast_to(device_row * per_dev + local_row, shape).reshape(N_ROWS, N_REP, -1)
    global_col = jnp.broadcast_to((section_step * N_REP + rep_index) * per_dev + local_col, shape).reshape(N_ROWS, N_REP, -1)
    flags = present[global_row, global_col].astype(jnp.int32)
    slot_total = global_row.shape[-1]
    ranking = (1 - flags) * slot_total + jnp.arange(slot_total)
    order = jnp.argsort(ranking, axis=-1)
    global_row = jnp.take_along_axis(global_row, order, axis=-1)[..., :KMAX]
    global_col = jnp.take_along_axis(global_col, order, axis=-1)[..., :KMAX]
    flags = jnp.take_along_axis(flags, order, axis=-1)[..., :KMAX]
    counts = jnp.sum(flags, axis=-1).astype(jnp.int32)
    pad_col = jnp.broadcast_to((jnp.arange(N_REP) * per_dev).reshape(1, N_REP, 1), global_col.shape)
    row_start = (jnp.arange(N_ROWS) * per_dev).reshape(N_ROWS, 1, 1)
    row_local = jnp.where(flags > 0, global_row - row_start, 0)
    col_kept = jnp.where(flags > 0, global_col, pad_col)
    row_degree = jnp.maximum(jnp.sum(present.astype(jnp.int32), axis=1), 1)
    return (row_local, col_kept, global_row, global_col, flags, counts, row_degree)


def draw_tile_coords(key, part):
    row_local, col_kept, global_row, global_col, flags, counts, row_degree = tile_layout(key)
    return jnp.stack([row_local, col_kept], axis=-1).astype(jnp.int32)


def draw_tile_count(key, part):
    row_local, col_kept, global_row, global_col, flags, counts, row_degree = tile_layout(key)
    return counts.astype(jnp.int32)


def draw_tiles(key, part):
    row_local, col_kept, global_row, global_col, flags, counts, row_degree = tile_layout(key)
    key = jax.random.fold_in(key, 11)
    tile_total = NODES // TILE
    lower = jnp.minimum(global_row, global_col)
    upper = jnp.maximum(global_row, global_col)
    identity = lower * tile_total + upper
    flipped = global_row > global_col
    diagonal = global_row == global_col
    degree_row = row_degree[global_row].astype(jnp.float32)
    degree_col = row_degree[global_col].astype(jnp.float32)
    factor = flags.astype(jnp.float32) / jnp.sqrt(TILE * jnp.sqrt(degree_row * degree_col))

    def one_tile(ident_one, flip_one, diag_one, factor_one):
        base = jax.random.normal(jax.random.fold_in(key, ident_one), (TILE, TILE), jnp.float32)
        base = jnp.where(diag_one, (base + base.T) * 0.70710678, base)
        base = jnp.where(flip_one, base.T, base)
        return base * factor_one

    def row_block(pieces):
        ident_row, flip_row, diag_row, factor_row = pieces
        made = jax.vmap(jax.vmap(one_tile))(ident_row, flip_row, diag_row, factor_row)
        return made.astype(jnp.bfloat16)
    return lax.map(row_block, (identity, flipped, diagonal, factor))


def block_levels(stream_key, shape, shards, low, high):
    gain, own = 1.0, jax.random.fold_in(stream_key, 6)
    for dim, parts in shards:
        heights = jnp.exp(jax.random.uniform(jax.random.fold_in(own, dim), (parts,), jnp.float32, low / len(shards), high / len(shards)))
        gain = gain * jnp.repeat(heights, shape[dim] // parts).reshape([-1 if axis == dim else 1 for axis in range(len(shape))])
    return gain


def centred(own_key, dims, width, limit, cuts=(), kind=jnp.bfloat16):
    gain = block_levels(own_key, dims, cuts, -0.22, 0.18) if cuts else 1.0
    values = jax.random.normal(own_key, dims, jnp.float32) * width * gain
    return jnp.minimum(jnp.maximum(values, -limit), limit).astype(kind)


def setup_inputs(seed: int = 0) -> dict:
    arg_keys = jax.random.split(jax.random.key(seed), 7)
    return {
        "features": centred(arg_keys[0], (NODES, F), 1.0, 6.0, ((0, 128),)),
        "weight": centred(arg_keys[1], (F, F), F ** -0.5, 0.375),
        "cotangent": centred(arg_keys[2], (NODES, F), 1.0, 6.0, ((0, 128),)),
        "tile_coords": draw_tile_coords(jax.random.fold_in(arg_keys[6], 71), 0),
        "tile_count": draw_tile_count(jax.random.fold_in(arg_keys[6], 71), 0),
        "tiles": draw_tiles(jax.random.fold_in(arg_keys[6], 71), 0),
    }


def dsilu(value):
    sigma = jax.nn.sigmoid(value)
    return sigma * (1.0 + value * (1.0 - sigma))

def reference(features, weight, cotangent, tile_coords, tile_count, tiles):
    per_dev = ROWS_DEV // TILE
    tile_total = NODES // TILE
    transformed = jnp.dot(features, weight, preferred_element_type=jnp.float32).astype(jnp.bfloat16)
    panels = transformed.reshape(tile_total, TILE, F)
    slot_ids = jnp.arange(KMAX, dtype=jnp.int32)

    def forward_block(pieces):
        coords, counts, values = pieces
        valid = (slot_ids[None, :] < counts[:, None]).reshape(-1).astype(jnp.float32)
        coords = coords.reshape(-1, 2)
        values = values.reshape(-1, TILE, TILE)
        gathered = panels[coords[:, 1]]
        product = jnp.einsum('kab,kbf->kaf', values.astype(jnp.float32), gathered.astype(jnp.float32))
        picker = (coords[:, 0][None, :] == jnp.arange(per_dev, dtype=jnp.int32)[:, None]).astype(jnp.float32) * valid[None, :]
        return jnp.einsum('rk,kaf->raf', picker, product, precision=lax.Precision.HIGHEST)
    aggregated = lax.map(forward_block, (tile_coords, tile_count, tiles)).reshape(NODES, F)
    activation = jax.nn.silu(aggregated).astype(jnp.bfloat16)
    slope = (cotangent.astype(jnp.float32) * dsilu(aggregated)).astype(jnp.bfloat16)
    slope_tiles = slope.reshape(tile_total, TILE, F)

    def backward_step(carry, pieces):
        coords, counts, values, block = pieces
        valid = (slot_ids[None, :] < counts[:, None]).reshape(-1).astype(jnp.float32)
        coords = coords.reshape(-1, 2)
        values = values.reshape(-1, TILE, TILE)
        source = slope_tiles[block * per_dev + coords[:, 0]]
        contrib = jnp.einsum('kba,kbf->kaf', values.astype(jnp.float32), source.astype(jnp.float32))
        contrib = contrib * valid[:, None, None]
        return (carry.at[coords[:, 1]].add(contrib), None)
    backward, _ = lax.scan(backward_step, jnp.zeros((tile_total, TILE, F), jnp.float32), (tile_coords, tile_count, tiles, jnp.arange(N_ROWS, dtype=jnp.int32)))
    back_rounded = backward.reshape(NODES, F).astype(jnp.bfloat16)
    input_grad = jnp.dot(back_rounded, weight.T, preferred_element_type=jnp.float32).astype(jnp.bfloat16)
    weight_grad = jnp.dot(features.T, back_rounded, preferred_element_type=jnp.float32) * (1.0 / math.sqrt(NODES))
    return (activation, input_grad, weight_grad)
```

```python
import functools
import math

import jax
import jax.numpy as jnp
from jax import lax
from jax.experimental import pallas as pl
from jax.experimental.pallas import tpu as pltpu
from jax.sharding import PartitionSpec as P

MESH = pl.DeviceIdType.MESH
NX, NY, NZ = 4, 8, 8
NS = NY // 2
HALF = NS * NZ
ROWS, F, TILE, KMAX = 256, 256, 128, 20
BF, F32 = jnp.bfloat16, jnp.float32


def at(x, y, z, k):
    return ((z * NY + y) * 2 + k, x)


def start(src, dst, send_sem, recv_sem, device):
    pltpu.make_async_remote_copy(
        src_ref=src, dst_ref=dst, send_sem=send_sem, recv_sem=recv_sem,
        device_id=device, device_id_type=MESH,
    ).start()


def wait(ref, sem):
    pltpu.make_async_copy(ref, ref, sem).wait()


def loop(low, high, body):
    def step(index, carry):
        body(index)
        return carry

    lax.fori_loop(low, high, step, 0)


class Place:
    def __init__(self):
        rows = lax.axis_index("rows")
        self.x = lax.axis_index("rep")
        self.k = rows % 2
        self.y = (rows // 2) % NY
        self.z = rows // (2 * NY)
        self.parity = self.x // 2
        self.owner = self.x % 2
        self.on_row = self.y % 2 == self.parity
        self.source = self.on_row & (self.k == self.owner)
        self.yy = self.y // 2


def z_near(me, o):
    step = jnp.where(o % 2 == 1, (o + 1) // 2, NZ - o // 2)
    return (me.z + step) % NZ


def row_near(me, m):
    on = jnp.where(m == 0, 0, jnp.where(m == 1, 2, jnp.where(m == 2, NY - 2, 4)))
    off = jnp.where(m == 0, NY - 1, jnp.where(m == 1, 1, jnp.where(m == 2, NY - 3, 3)))
    return ((me.y + jnp.where(me.on_row, on, off)) % NY) // 2


def gather_begin(me, pan, recv, sent):
    @pl.when(me.source)
    def _():
        first = me.yy * NZ + me.z
        second = me.z * NS + me.yy

        def along(o):
            start(pan.at[first], pan.at[first], sent, recv.at[first],
                  at(me.x, me.y, z_near(me, o), 0))
            step = jnp.where(o % 2 == 1, (o + 1) // 2, NY - o // 2)
            start(pan.at[HALF + second], pan.at[HALF + second], sent, recv.at[second],
                  at(me.x, (me.y + step) % NY, me.z, 1))

        loop(1, NZ, along)

        @pl.when(me.owner == 1)
        def _():
            start(pan.at[first], pan.at[first], sent, recv.at[first], at(me.x, me.y, me.z, 0))

        @pl.when(me.owner == 0)
        def _():
            start(pan.at[HALF + second], pan.at[HALF + second], sent, recv.at[second],
                  at(me.x, me.y, me.z, 1))


def gather_first(me, pan, recv, sent, pair):
    up = at(me.x, (me.y + 1) % NY, me.z, 0)
    down = at(me.x, (me.y + NY - 1) % NY, me.z, 0)

    def send(slot, device):
        start(pan.at[slot], pan.at[slot], sent, recv.at[slot], device)

    def share(slot):
        start(pan.at[slot], pan.at[slot], sent, pair, at(me.x, me.y, me.z, 1))

    def arrived(slot):
        wait(pan.at[slot], recv.at[slot])

    @pl.when(me.on_row)
    def _():
        def own(o):
            slot = me.yy * NZ + z_near(me, o)

            @pl.when((o > 0) | (me.owner == 1))
            def _():
                arrived(slot)

            send(slot, up)
            send(slot, down)

            @pl.when((o > 0) | (me.owner == 0))
            def _():
                share(slot)

        loop(0, NZ, own)

        def near(o):
            zs = z_near(me, o)
            below = ((me.yy + NS - 1) % NS) * NZ + zs
            arrived(below)
            send(below, up)
            share(below)
            above = ((me.yy + 1) % NS) * NZ + zs
            arrived(above)
            send(above, down)
            share(above)

        loop(0, NZ, near)

        def far(o):
            slot = ((me.yy + 2) % NS) * NZ + z_near(me, o)
            arrived(slot)
            share(slot)

        loop(0, NZ, far)

    @pl.when(jnp.logical_not(me.on_row))
    def _():
        skew = 3

        def step(t):
            @pl.when(t < NZ)
            def _():
                zs = z_near(me, t)
                below = (((me.y + NY - 1) % NY) // 2) * NZ + zs
                arrived(below)
                send(below, up)
                share(below)
                above = (((me.y + 1) % NY) // 2) * NZ + zs
                arrived(above)
                send(above, down)
                share(above)

            @pl.when(t >= skew)
            def _():
                o = t - skew
                zs = z_near(me, o)
                below = (((me.y + NY - 3) % NY) // 2) * NZ + zs
                arrived(below)

                @pl.when(o % 2 == 0)
                def _():
                    send(below, up)

                share(below)
                above = (((me.y + 3) % NY) // 2) * NZ + zs
                arrived(above)

                @pl.when(o % 2 == 1)
                def _():
                    send(above, down)

                share(above)

        loop(0, NZ + skew, step)


def gather_second(me, pan, recv, sent, pair):
    up = at(me.x, me.y, (me.z + 1) % NZ, 1)
    down = at(me.x, me.y, (me.z + NZ - 1) % NZ, 1)

    def send(slot, device):
        start(pan.at[HALF + slot], pan.at[HALF + slot], sent, recv.at[slot], device)

    def share(slot):
        start(pan.at[HALF + slot], pan.at[HALF + slot], sent, pair, at(me.x, me.y, me.z, 0))

    def arrived(slot):
        wait(pan.at[HALF + slot], recv.at[slot])

    def own(m):
        slot = me.z * NS + row_near(me, m)
        mine = me.on_row & (m == 0)

        @pl.when(jnp.logical_not(mine & (me.owner == 1)))
        def _():
            arrived(slot)

        send(slot, up)
        send(slot, down)

        @pl.when(jnp.logical_not(mine & (me.owner == 0)))
        def _():
            share(slot)

    loop(0, NS, own)

    def onward(t):
        distance = 1 + t // NS
        m = t % NS
        row = row_near(me, m)
        below = ((me.z + NZ - distance) % NZ) * NS + row
        arrived(below)

        @pl.when((distance < 3) | (m % 2 == 0))
        def _():
            send(below, up)

        share(below)
        above = ((me.z + distance) % NZ) * NS + row
        arrived(above)

        @pl.when((distance < 3) | (m % 2 == 1))
        def _():
            send(above, down)

        share(above)

    loop(0, 3 * NS, onward)

    def last(m):
        slot = ((me.z + 4) % NZ) * NS + row_near(me, m)
        arrived(slot)
        share(slot)

    loop(0, NS, last)


def gather(me, pan, recv, sent, pair):
    @pl.when(me.k == 0)
    def _():
        gather_first(me, pan, recv, sent, pair)

    @pl.when(me.k == 1)
    def _():
        gather_second(me, pan, recv, sent, pair)

    @pl.when(me.source)
    def _():
        wait(pan.at[pl.ds(0, HALF - 1)], pair)

    @pl.when(jnp.logical_not(me.source))
    def _():
        wait(pan.at[pl.ds(0, HALF)], pair)


def gather_end(me, pan, sent):
    first = jnp.where(me.on_row, 4 * NZ, 3 * NZ)
    second = 7 * NS
    count = jnp.where(me.k == 0, first, second) + HALF
    count = count - jnp.where(me.on_row & (me.k != me.owner), 1, 0)
    count = count + jnp.where(me.source, 2 * (NZ - 1) + 1, 0)
    loop(0, count, lambda i: wait(pan.at[0], sent))


def aggregate(coords, lhs, pan, rhs):
    def pick(i):
        column = coords[0, 0, i, 1]
        section = column // 8
        slot = jnp.where(column % 2 == 0, (section % NS) * NZ + section // NS, HALF + section)
        rhs[pl.ds(pl.multiple_of(i * TILE, TILE), TILE), :] = pan[slot]

    loop(0, KMAX, pick)
    return jnp.dot(lhs[...], rhs[...], preferred_element_type=F32)


def kernel(features, weight, cotangent, coords, tiles, act_ref, grad_ref, wg_ref,
           pan1, pan2, lhs, rhs, hx, slope_ref, wgp, wy, wz, wall, bp, bx, ig,
           recv1, recv2, sent1, sent2, pair1, pair2, hx_recv, hx_sent,
           wy_recv, wz_recv, wq_recv, wx_recv, w_sent, wx_sent, bx_recv, ig_recv, b_sent):
    me = Place()
    x, y, z, k = me.x, me.y, me.z, me.k

    barrier = pltpu.get_barrier_semaphore()

    def hello(d):
        for core in range(2):
            pl.semaphore_signal(barrier, inc=1, device_id=at(x, (y + d) % NY, z, core),
                                device_id_type=MESH)
            pl.semaphore_signal(barrier, inc=1, device_id=at(x, y, (z + d) % NZ, core),
                                device_id_type=MESH)

    loop(1, NY, hello)
    for d in range(1, NX):
        pl.semaphore_signal(barrier, inc=1, device_id=at((x + d) % NX, y, z, k),
                            device_id_type=MESH)
    pl.semaphore_signal(barrier, inc=1, device_id=at(x, y, z, 1 - k), device_id_type=MESH)

    @pl.when(me.source)
    def _():
        pan1[me.yy * NZ + z] = features[0:TILE, :]
        pan1[HALF + z * NS + me.yy] = features[TILE:, :]

    pl.semaphore_wait(barrier, 4 * (NY - 1) + NX)

    gather_begin(me, pan1, recv1, sent1)

    def lay(i):
        row = coords[0, 0, i, 0]
        tile = tiles[0, 0, i]
        columns = pl.ds(pl.multiple_of(i * TILE, TILE), TILE)
        zero = jnp.zeros_like(tile)
        lhs[0:TILE, columns] = jnp.where(row == 0, tile, zero)
        lhs[TILE:, columns] = jnp.where(row == 0, zero, tile)

    loop(0, KMAX, lay)

    gather(me, pan1, recv1, sent1, pair1)
    hx[x] = aggregate(coords, lhs, pan1, rhs).astype(BF)

    home = 2 * (y % 2) + k

    def give(d):
        to = (home + d) % NX

        @pl.when(to != x)
        def _():
            start(hx.at[x], hx.at[x], hx_sent, hx_recv.at[x], at(to, y, z, k))

    loop(0, NX, give)

    def middle():
        def take(d):
            wait(hx.at[(x + d) % NX], hx_recv.at[(x + d) % NX])

        loop(1, NX, take)
        hidden = (hx[0].astype(F32) + hx[1].astype(F32)) + (hx[2].astype(F32) + hx[3].astype(F32))
        hidden = hidden.astype(BF)
        hx[x] = hidden
        v = jnp.dot(hidden, weight[...], preferred_element_type=F32)
        s = 1.0 / (1.0 + jnp.exp(-v))
        slope_ref[...] = (cotangent[...].astype(F32) * (s * (1.0 + v * (1.0 - s)))).astype(BF)
        act_ref[...] = (v * s).astype(BF)

    def hx_done():
        loop(1, NX, lambda d: wait(hx.at[0], hx_sent))

    hx_done()

    @pl.when(me.source)
    def _():
        middle()
        pan2[me.yy * NZ + z] = slope_ref[0:TILE, :]
        pan2[HALF + z * NS + me.yy] = slope_ref[TILE:, :]

    gather_begin(me, pan2, recv2, sent2)
    gather(me, pan2, recv2, sent2, pair2)

    @pl.when(jnp.logical_not(me.source))
    def _():
        middle()

    term = lax.dot_general(hx[x], slope_ref[...], (((0,), (0,)), ((), ())),
                           preferred_element_type=F32)
    wgp[0] = term[:, 0:TILE]
    wgp[1] = term[:, TILE:]
    mine = y * 2 + k

    def chunk(to):
        return wgp.at[to % 2, pl.ds(pl.multiple_of(x * 64 + (to // 2) * 8, 8), 8), :]

    def scatter_y(d):
        to = (mine + d) % 16
        start(chunk(to), wy.at[mine], w_sent, wy_recv.at[mine], at(x, to // 2, z, to % 2))

    loop(1, 16, scatter_y)
    wy[mine] = chunk(mine)[...]

    back = aggregate(coords, lhs, pan2, rhs)
    bp[...] = back.astype(BF).reshape(NX, 64, F)

    def give_back(d):
        to = (x + d) % NX
        start(bp.at[to], bx.at[x], b_sent, bx_recv.at[x], at(to, y, z, k))

    loop(1, NX, give_back)
    bx[x] = bp[x]

    def take_y(d):
        src = (mine + d) % 16
        wait(wy.at[src], wy_recv.at[src])

    loop(1, 16, take_y)
    wz[z] = jnp.sum(wy[...], axis=0)

    def scatter_z(d):
        start(wz.at[z], wz.at[z], w_sent, wz_recv.at[z], at(x, y, (z + d) % NZ, k))

    loop(1, NZ, scatter_z)

    def take_back(d):
        wait(bx.at[(x + d) % NX], bx_recv.at[(x + d) % NX])

    loop(1, NX, take_back)
    total = (bx[0].astype(F32) + bx[1].astype(F32)) + (bx[2].astype(F32) + bx[3].astype(F32))
    ig[x] = lax.dot_general(total.astype(BF), weight[...], (((1,), (1,)), ((), ())),
                            preferred_element_type=F32).astype(BF)

    def give_grad(d):
        start(ig.at[x], ig.at[x], b_sent, ig_recv.at[x], at((x + d) % NX, y, z, k))

    loop(1, NX, give_grad)

    def take_z(d):
        src = (z + d) % NZ
        wait(wz.at[src], wz_recv.at[src])

    loop(1, NZ, take_z)
    wall[x, mine] = jnp.sum(wz[...], axis=0) * (1.0 / math.sqrt(ROWS * NY * NZ * 2))

    def spread_y(d):
        to = (mine + d) % 16
        start(wall.at[x, mine], wall.at[x, mine], w_sent, wq_recv.at[mine],
              at(x, to // 2, z, to % 2))

    loop(1, 16, spread_y)

    def take_grad(d):
        wait(ig.at[(x + d) % NX], ig_recv.at[(x + d) % NX])

    loop(1, NX, take_grad)
    grad_ref[...] = ig[...].reshape(ROWS, F)

    def take_q(d):
        src = (mine + d) % 16
        wait(wall.at[x, src], wq_recv.at[src])

    loop(1, 16, take_q)

    def spread_x(d):
        start(wall.at[x], wall.at[x], wx_sent, wx_recv.at[x], at((x + d) % NX, y, z, k))

    loop(1, NX, spread_x)

    gather_end(me, pan1, sent1)
    gather_end(me, pan2, sent2)
    loop(0, 15 + 7 + 15, lambda i: wait(wz.at[0], w_sent))
    loop(0, 6, lambda i: wait(bp.at[0], b_sent))

    def take_x(d):
        wait(wall.at[(x + d) % NX], wx_recv.at[(x + d) % NX])

    loop(1, NX, take_x)
    loop(1, NX, lambda d: wait(wall.at[0], wx_sent))
    for quarter in range(NX):
        for row in range(8):
            for half in range(2):
                wg_ref[quarter * 64 + row * 8:quarter * 64 + row * 8 + 8,
                       half * TILE:(half + 1) * TILE] = wall[quarter, row * 2 + half]


def on_device(features, weight, cotangent, tile_coords, tile_count, tiles):
    vmem = pl.BlockSpec(memory_space=pltpu.VMEM)
    smem = pl.BlockSpec(memory_space=pltpu.SMEM)
    dma = pltpu.SemaphoreType.DMA
    return pl.pallas_call(
        kernel,
        out_shape=(
            jax.ShapeDtypeStruct((ROWS, F), BF),
            jax.ShapeDtypeStruct((ROWS, F), BF),
            jax.ShapeDtypeStruct((F, F), F32),
        ),
        in_specs=[vmem, vmem, vmem, smem, vmem],
        out_specs=(vmem, vmem, vmem),
        scratch_shapes=[
            pltpu.VMEM((2 * HALF, TILE, F), BF),
            pltpu.VMEM((2 * HALF, TILE, F), BF),
            pltpu.VMEM((2 * TILE, KMAX * TILE), BF),
            pltpu.VMEM((KMAX * TILE, F), BF),
            pltpu.VMEM((NX, ROWS, F), BF),
            pltpu.VMEM((ROWS, F), BF),
            pltpu.VMEM((2, F, TILE), F32),
            pltpu.VMEM((16, 8, TILE), F32),
            pltpu.VMEM((NZ, 8, TILE), F32),
            pltpu.VMEM((NX, 16, 8, TILE), F32),
            pltpu.VMEM((NX, 64, F), BF),
            pltpu.VMEM((NX, 64, F), BF),
            pltpu.VMEM((NX, 64, F), BF),
            dma((HALF,)), dma((HALF,)), dma(()), dma(()), dma(()), dma(()),
            dma((NX,)), dma(()),
            dma((16,)), dma((NZ,)), dma((16,)), dma((NX,)), dma(()), dma(()),
            dma((NX,)), dma((NX,)), dma(()),
        ],
        compiler_params=pltpu.CompilerParams(
            collective_id=0, has_side_effects=True, vmem_limit_bytes=40 << 20
        ),
        name="graph_layer",
    )(features, weight, cotangent, tile_coords, tiles)


def solution(mesh):
    placed = (
        P("rows", None),
        P(),
        P("rows", None),
        P("rows", "rep", None, None),
        P("rows", "rep"),
        P("rows", "rep", None, None, None),
    )
    return jax.shard_map(
        on_device,
        mesh=mesh,
        in_specs=placed,
        out_specs=(P("rows", None), P("rows", None), P()),
        check_vma=False,
    )
```

```python
import math

import jax
import jax.numpy as jnp
from jax import lax
from jax.experimental import pallas as pl
from jax.experimental.pallas import tpu as pltpu
from jax.sharding import PartitionSpec as P

MESH = pl.DeviceIdType.MESH
NX, NY, NZ = 4, 8, 8
NS = NY // 2
HALF = NS * NZ
ROWS, F, TILE, KMAX = 256, 256, 128, 20
BF, F32 = jnp.bfloat16, jnp.float32

PARTS = 1
ROOT = (
    ((0, 3), (0, -3), (0, 2), (0, -2), (0, 1), (0, -1), (0, 4), (1, 0), (-1, 0)),
    ((3, 0), (-3, 0), (2, 0), (-2, 0), (1, 0), (-1, 0), (4, 0), (0, 1), (0, -1)),
)
STEPS = {
    (0, True): (
        (0,0,1,(1,0),(-1,0)), (0,0,-1,(1,0),(-1,0)), (0,0,2,(1,0),(-1,0)), (0,0,-2,(1,0),(-1,0)),
        (0,0,3,(1,0),(-1,0)), (0,0,-3,(1,0),(-1,0)), (0,0,4,(1,0),(-1,0)), (0,2,0,(1,0)), (0,-2,0,(-1,0)),
        (0,2,1,(1,0)), (0,-2,1,(-1,0)), (0,2,-1,(1,0)), (0,2,2,(1,0)), (0,-2,-1,(-1,0)), (0,-2,2,(-1,0)),
        (0,2,-2,(1,0)), (0,2,3,(1,0)), (0,-2,-2,(-1,0)), (0,-2,3,(-1,0)), (0,2,-3,(1,0)), (0,-2,-3,(-1,0)),
        (0,2,4,(1,0)), (0,-2,4,(-1,0)), (0,4,0), (0,4,1), (0,4,-1), (0,4,2), (0,4,-2), (0,4,3), (0,4,-3),
        (0,4,4),
    ),
    (0, False): (
        (0,1,0,(1,0)), (0,-1,0,(-1,0)), (0,1,1,(1,0)), (0,-1,1,(-1,0)), (0,1,-1,(1,0)), (0,1,2,(1,0)),
        (0,1,-2,(1,0)), (0,1,3,(1,0)), (0,-1,-1,(-1,0)), (0,-1,2,(-1,0)), (0,-1,-2,(-1,0)), (0,-1,3,(-1,0)),
        (0,1,-3,(1,0)), (0,-1,-3,(-1,0)), (0,1,4,(1,0)), (0,-1,4,(-1,0)), (0,3,0,(1,0)), (0,-3,0),
        (0,3,1,(1,0)), (0,-3,1), (0,3,-1,(1,0)), (0,3,2,(1,0)), (0,-3,-1), (0,-3,2), (0,3,-2,(1,0)),
        (0,3,3,(1,0)), (0,-3,-2), (0,-3,3), (0,3,-3,(1,0)), (0,-3,-3), (0,3,4,(1,0)), (0,-3,4),
    ),
    (1, True): (
        (1,2,0,(0,1),(0,-1)), (1,-2,0,(0,1),(0,-1)), (1,0,1,(0,1)), (1,0,-1,(0,-1)), (1,4,0,(0,1),(0,-1)),
        (1,2,1,(0,1)), (1,-2,1,(0,1)), (1,2,-1,(0,-1)), (1,-2,-1,(0,-1)), (1,0,2,(0,1)), (1,0,-2,(0,-1)),
        (1,4,1,(0,1)), (1,4,-1,(0,-1)), (1,2,2,(0,1)), (1,-2,2,(0,1)), (1,2,-2,(0,-1)), (1,-2,-2,(0,-1)),
        (1,0,3,(0,1)), (1,0,-3), (1,4,2,(0,1)), (1,4,-2,(0,-1)), (1,2,3,(0,1)), (1,-2,3,(0,1)), (1,2,-3),
        (1,-2,-3), (1,0,4), (1,4,3,(0,1)), (1,4,-3), (1,2,4), (1,-2,4), (1,4,4),
    ),
    (1, False): (
        (1,1,0,(0,1),(0,-1)), (1,-1,0,(0,1),(0,-1)), (1,3,0,(0,1),(0,-1)), (1,-3,0,(0,1),(0,-1)),
        (1,1,1,(0,1)), (1,-1,1,(0,1)), (1,1,-1,(0,-1)), (1,3,1,(0,1)), (1,-1,-1,(0,-1)), (1,3,-1,(0,-1)),
        (1,-3,1,(0,1)), (1,-3,-1,(0,-1)), (1,1,2,(0,1)), (1,-1,2,(0,1)), (1,1,-2,(0,-1)), (1,-1,-2,(0,-1)),
        (1,3,2,(0,1)), (1,-3,2,(0,1)), (1,3,-2,(0,-1)), (1,-3,-2,(0,-1)), (1,1,3,(0,1)), (1,-1,3,(0,1)),
        (1,1,-3), (1,-1,-3), (1,3,3,(0,1)), (1,-3,3,(0,1)), (1,3,-3), (1,-3,-3), (1,1,4), (1,-1,4), (1,3,4),
        (1,-3,4),
    ),
}
PIECE = TILE // PARTS


def at(x, y, z, k):
    return ((z * NY + y) * 2 + k, x)


def start(src, dst, send_sem, recv_sem, device):
    pltpu.make_async_remote_copy(
        src_ref=src, dst_ref=dst, send_sem=send_sem, recv_sem=recv_sem,
        device_id=device, device_id_type=MESH,
    ).start()


def wait(ref, sem):
    pltpu.make_async_copy(ref, ref, sem).wait()


def loop(low, high, body):
    def step(index, carry):
        body(index)
        return carry

    lax.fori_loop(low, high, step, 0)


class Place:
    def __init__(self):
        rows = lax.axis_index("rows")
        self.x = lax.axis_index("rep")
        self.k = rows % 2
        self.y = (rows // 2) % NY
        self.z = rows // (2 * NY)
        self.owner = self.x % 2
        self.on_row = self.y % 2 == self.x // 2
        self.source = self.on_row & (self.k == self.owner)
        self.panel = self.z * NS + self.y // 2


class Gather:
    def __init__(self, me, pan, recv, sent, pair):
        self.me, self.pan, self.recv, self.sent, self.pair = me, pan, recv, sent, pair

    def piece(self, p, panel):
        return self.pan.at[(p % 2) * HALF + panel, pl.ds((p // 2) * PIECE, PIECE)]

    def send(self, p, panel, dy, dz):
        ref = self.piece(p, panel)
        device = at(self.me.x, (self.me.y + dy + NY) % NY, (self.me.z + dz + NZ) % NZ, p % 2)
        start(ref, ref, self.sent, self.recv.at[p * HALF + panel], device)

    def begin(self):
        me, pan = self.me, self.pan

        @pl.when(me.source)
        def _():
            sign = 1 - 2 * (me.z % 2)
            for turn in range(max(len(moves) for moves in ROOT)):
                for p, moves in enumerate(ROOT):
                    if turn < len(moves):
                        dy, dz = moves[turn]
                        self.send(p, me.panel, sign * dy, sign * dz)
            for half in range(2):
                ref = pan.at[half * HALF + me.panel]
                start(ref, ref, self.sent, self.pair, at(me.x, me.y, me.z, 1 - me.k))

    def forward(self, low, high):
        me = self.me
        for (core, on_row), steps in STEPS.items():
            part = steps[round(low * len(steps)):round(high * len(steps))]

            @pl.when((me.k == core) & (me.on_row == on_row))
            def _(part=part):
                for p, dy, dz, *moves in part:
                    sign = 1 - 2 * ((me.z + dz) % 2)
                    z = (me.z - sign * dz + NZ) % NZ
                    y = (me.y - sign * dy + NY) % NY
                    panel = z * NS + y // 2
                    ref = self.piece(p, panel)
                    wait(ref, self.recv.at[p * HALF + panel])
                    for my, mz in moves:
                        self.send(p, panel, sign * my, sign * mz)
                    start(ref, ref, self.sent, self.pair, at(me.x, me.y, me.z, 1 - me.k))

    def finish(self):
        me = self.me

        @pl.when(me.source)
        def _():
            wait(self.pan.at[pl.ds(0, HALF - 1)], self.pair)

        @pl.when(me.on_row & jnp.logical_not(me.source))
        def _():
            wait(self.pan.at[pl.ds(0, HALF + 1)], self.pair)

        @pl.when(jnp.logical_not(me.on_row))
        def _():
            wait(self.pan.at[pl.ds(0, HALF)], self.pair)

    def end(self):
        me = self.me
        count = jnp.where(me.source, sum(len(moves) for moves in ROOT) + 2 * PARTS, 0)
        for (core, on_row), steps in STEPS.items():
            total = sum(len(step) - 2 for step in steps)
            count = count + jnp.where((me.k == core) & (me.on_row == on_row), total, 0)
        loop(0, count, lambda i: wait(self.piece(0, 0), self.sent))


def aggregate(coords, lhs, pan, rhs):
    def pick(i):
        column = coords[0, 0, 1, i]
        slot = (column % 2) * HALF + column // 8
        rhs[pl.ds(pl.multiple_of(i * TILE, TILE), TILE), :] = pan[slot]

    loop(0, KMAX, pick)
    return jnp.dot(lhs[...], rhs[...], preferred_element_type=F32)


def kernel(features, weight_in, cotangent_in, coords, tiles_in, act_ref, grad_ref, wg_ref,
           pan1, pan2, weight, cotangent, tiles, lhs, rhs, hx, hid, slope_ref,
           wgp, wy, wz, wall, bp, bx, ig,
           f_sem, w_sem, c_sem, t_sem, recv1, recv2, sent1, sent2, pair1, pair2, hx_recv, hx_sent,
           wy_recv, wz_recv, wq_recv, wx_recv, w_sent, wx_sent, bx_recv, ig_recv, b_sent):
    me = Place()
    x, y, z, k = me.x, me.y, me.z, me.k

    own = [
        pltpu.make_async_copy(features.at[pl.ds(half * TILE, TILE)],
                              pan1.at[half * HALF + me.panel], f_sem.at[half])
        for half in range(2)
    ]

    @pl.when(me.source)
    def _():
        own[0].start()
        own[1].start()

    tiles_copy = pltpu.make_async_copy(tiles_in.at[0, 0], tiles, t_sem)
    tiles_copy.start()
    weight_copy = pltpu.make_async_copy(weight_in, weight, w_sem)
    weight_copy.start()
    cotangent_copy = pltpu.make_async_copy(cotangent_in, cotangent, c_sem)
    cotangent_copy.start()

    barrier = pltpu.get_barrier_semaphore()

    def hello(d):
        for core in range(2):
            pl.semaphore_signal(barrier, inc=1, device_id=at(x, (y + d) % NY, z, core),
                                device_id_type=MESH)
            pl.semaphore_signal(barrier, inc=1, device_id=at(x, y, (z + d) % NZ, core),
                                device_id_type=MESH)

    loop(1, NY, hello)
    for d in range(1, NX):
        pl.semaphore_signal(barrier, inc=1, device_id=at((x + d) % NX, y, z, k),
                            device_id_type=MESH)
    pl.semaphore_signal(barrier, inc=1, device_id=at(x, y, z, 1 - k), device_id_type=MESH)

    @pl.when(me.source)
    def _():
        own[0].wait()
        own[1].wait()

    pl.semaphore_wait(barrier, 4 * (NY - 1) + NX)

    one = Gather(me, pan1, recv1, sent1, pair1)
    two = Gather(me, pan2, recv2, sent2, pair2)
    one.begin()

    tiles_copy.wait()

    def lay(i):
        row = coords[0, 0, 0, i]
        tile = tiles[i]
        columns = pl.ds(pl.multiple_of(i * TILE, TILE), TILE)
        zero = jnp.zeros_like(tile)
        lhs[0:TILE, columns] = jnp.where(row == 0, tile, zero)
        lhs[TILE:, columns] = jnp.where(row == 0, zero, tile)

    loop(0, KMAX, lay)
    weight_copy.wait()
    cotangent_copy.wait()

    one.forward(0, 1)
    one.finish()
    hx[x] = aggregate(coords, lhs, pan1, rhs).astype(BF)

    home = 2 * (y % 2) + k

    def give(d):
        to = (home + d) % NX

        @pl.when(to != x)
        def _():
            start(hx.at[x], hx.at[x], hx_sent, hx_recv.at[x], at(to, y, z, k))

    loop(0, NX, give)

    def middle():
        def take(d):
            wait(hx.at[(x + d) % NX], hx_recv.at[(x + d) % NX])

        loop(1, NX, take)
        hidden = (hx[0].astype(F32) + hx[1].astype(F32)) + (hx[2].astype(F32) + hx[3].astype(F32))
        hid[...] = hidden.astype(BF)
        v = jnp.dot(hid[...], weight[...], preferred_element_type=F32)
        s = 1.0 / (1.0 + jnp.exp(-v))
        slope_ref[...] = (cotangent[...].astype(F32) * (s * (1.0 + v * (1.0 - s)))).astype(BF)
        act_ref[...] = (v * s).astype(BF)

    @pl.when(me.source)
    def _():
        middle()
        pan2[me.panel] = slope_ref[0:TILE, :]
        pan2[HALF + me.panel] = slope_ref[TILE:, :]

    two.begin()
    two.forward(0, CUTS[0])

    @pl.when(jnp.logical_not(me.source))
    def _():
        middle()

    term = lax.dot_general(hid[...], slope_ref[...], (((0,), (0,)), ((), ())),
                           preferred_element_type=F32)
    wgp[0] = term[:, 0:TILE]
    wgp[1] = term[:, TILE:]
    mine = y * 2 + k

    def chunk(to):
        return wgp.at[to % 2, pl.ds(pl.multiple_of(x * 64 + (to // 2) * 8, 8), 8), :]

    def scatter_y(d):
        to = (mine + d) % 16
        start(chunk(to), wy.at[mine], w_sent, wy_recv.at[mine], at(x, to // 2, z, to % 2))

    loop(1, 16, scatter_y)
    wy[mine] = chunk(mine)[...]

    two.forward(CUTS[0], CUTS[1])

    def take_y(d):
        src = (mine + d) % 16
        wait(wy.at[src], wy_recv.at[src])

    loop(1, 16, take_y)
    wz[z] = jnp.sum(wy[...], axis=0)

    def scatter_z(d):
        start(wz.at[z], wz.at[z], w_sent, wz_recv.at[z], at(x, y, (z + d) % NZ, k))

    loop(1, NZ, scatter_z)

    two.forward(CUTS[1], CUTS[2])

    def take_z(d):
        src = (z + d) % NZ
        wait(wz.at[src], wz_recv.at[src])

    loop(1, NZ, take_z)
    wall[x, mine] = jnp.sum(wz[...], axis=0) * (1.0 / math.sqrt(ROWS * NY * NZ * 2))

    def spread_y(d):
        to = (mine + d) % 16
        start(wall.at[x, mine], wall.at[x, mine], w_sent, wq_recv.at[mine],
              at(x, to // 2, z, to % 2))

    loop(1, 16, spread_y)

    two.forward(CUTS[2], 1)
    two.finish()

    bp[...] = aggregate(coords, lhs, pan2, rhs).astype(BF).reshape(NX, 64, F)

    def give_back(d):
        to = (x + d) % NX
        start(bp.at[to], bx.at[x], b_sent, bx_recv.at[x], at(to, y, z, k))

    loop(1, NX, give_back)
    bx[x] = bp[x]

    def take_q(d):
        src = (mine + d) % 16
        wait(wall.at[x, src], wq_recv.at[src])

    loop(1, 16, take_q)

    def spread_x(d):
        start(wall.at[x], wall.at[x], wx_sent, wx_recv.at[x], at((x + d) % NX, y, z, k))

    loop(1, NX, spread_x)

    def take_back(d):
        wait(bx.at[(x + d) % NX], bx_recv.at[(x + d) % NX])

    loop(1, NX, take_back)
    total = (bx[0].astype(F32) + bx[1].astype(F32)) + (bx[2].astype(F32) + bx[3].astype(F32))
    ig[x] = lax.dot_general(total.astype(BF), weight[...], (((1,), (1,)), ((), ())),
                            preferred_element_type=F32).astype(BF)

    def give_grad(d):
        start(ig.at[x], ig.at[x], b_sent, ig_recv.at[x], at((x + d) % NX, y, z, k))

    loop(1, NX, give_grad)

    one.end()
    two.end()
    loop(1, NX, lambda d: wait(hx.at[0], hx_sent))
    loop(0, 15 + 7 + 15, lambda i: wait(wz.at[0], w_sent))

    def take_x(d):
        wait(wall.at[(x + d) % NX], wx_recv.at[(x + d) % NX])

    loop(1, NX, take_x)
    for quarter in range(NX):
        for row in range(8):
            for half in range(2):
                wg_ref[quarter * 64 + row * 8:quarter * 64 + row * 8 + 8,
                       half * TILE:(half + 1) * TILE] = wall[quarter, row * 2 + half]

    def take_grad(d):
        wait(ig.at[(x + d) % NX], ig_recv.at[(x + d) % NX])

    loop(1, NX, take_grad)
    grad_ref[...] = ig[...].reshape(ROWS, F)
    loop(1, NX, lambda d: wait(wall.at[0], wx_sent))
    loop(0, 6, lambda i: wait(bp.at[0], b_sent))


CUTS = (0.3, 0.55, 0.8)


def on_device(features, weight, cotangent, tile_coords, tile_count, tiles):
    vmem = pl.BlockSpec(memory_space=pltpu.VMEM)
    smem = pl.BlockSpec(memory_space=pltpu.SMEM)
    anywhere = pl.BlockSpec(memory_space=pl.ANY)
    dma = pltpu.SemaphoreType.DMA
    return pl.pallas_call(
        kernel,
        out_shape=(
            jax.ShapeDtypeStruct((ROWS, F), BF),
            jax.ShapeDtypeStruct((ROWS, F), BF),
            jax.ShapeDtypeStruct((F, F), F32),
        ),
        in_specs=[anywhere, anywhere, anywhere, smem, anywhere],
        out_specs=(vmem, vmem, vmem),
        scratch_shapes=[
            pltpu.VMEM((2 * HALF, TILE, F), BF),
            pltpu.VMEM((2 * HALF, TILE, F), BF),
            pltpu.VMEM((F, F), BF),
            pltpu.VMEM((ROWS, F), BF),
            pltpu.VMEM((KMAX, TILE, TILE), BF),
            pltpu.VMEM((2 * TILE, KMAX * TILE), BF),
            pltpu.VMEM((KMAX * TILE, F), BF),
            pltpu.VMEM((NX, ROWS, F), BF),
            pltpu.VMEM((ROWS, F), BF),
            pltpu.VMEM((ROWS, F), BF),
            pltpu.VMEM((2, F, TILE), F32),
            pltpu.VMEM((16, 8, TILE), F32),
            pltpu.VMEM((NZ, 8, TILE), F32),
            pltpu.VMEM((NX, 16, 8, TILE), F32),
            pltpu.VMEM((NX, 64, F), BF),
            pltpu.VMEM((NX, 64, F), BF),
            pltpu.VMEM((NX, 64, F), BF),
            dma((2,)), dma(()), dma(()), dma(()),
            dma((2 * PARTS * HALF,)), dma((2 * PARTS * HALF,)), dma(()), dma(()), dma(()), dma(()),
            dma((NX,)), dma(()),
            dma((16,)), dma((NZ,)), dma((16,)), dma((NX,)), dma(()), dma(()),
            dma((NX,)), dma((NX,)), dma(()),
        ],
        compiler_params=pltpu.CompilerParams(
            collective_id=0, has_side_effects=True, vmem_limit_bytes=60 << 20
        ),
        name="graph_layer",
    )(features, weight, cotangent, jnp.swapaxes(tile_coords, 2, 3), tiles)


def solution(mesh):
    placed = (
        P("rows", None),
        P(),
        P("rows", None),
        P("rows", "rep", None, None),
        P("rows", "rep"),
        P("rows", "rep", None, None, None),
    )
    return jax.shard_map(
        on_device,
        mesh=mesh,
        in_specs=placed,
        out_specs=(P("rows", None), P("rows", None), P()),
        check_vma=False,
    )
```

```python
import math

import jax
import jax.numpy as jnp
from jax import lax
from jax.experimental import pallas as pl
from jax.experimental.pallas import tpu as pltpu
from jax.sharding import PartitionSpec as P

MESH = pl.DeviceIdType.MESH
NX, NY, NZ = 4, 8, 8
NS = NY // 2
HALF = NS * NZ
ROWS, F, TILE, KMAX = 256, 256, 128, 20
BF, F32 = jnp.bfloat16, jnp.float32

PARTS = 1
ROOT = (
    ((-1,0), (0,1), (0,-3), (2,0), (1,0),),
    ((0,1), (3,0), (0,-2), (-1,0), (-2,0), (0,-1), (0,2), (1,0),),
)
STEPS = {
    (0, True): (
        (0,0,1,(-2,0),(0,1)), (0,2,0,(0,3),(0,1),(1,0),(0,-1)), (0,0,-3,(1,0),(0,1),(0,-1)), (0,-2,0),
        (0,-2,1,(-1,0),(0,1)), (0,0,2,(-1,0),(0,1)), (0,2,1,(1,0)), (0,2,3,(0,-1),(1,0),(-1,0)),
        (0,2,-1,(0,-1)), (0,-2,-1), (0,0,4,(-1,0)), (0,0,-2,(1,0)), (0,0,-1), (0,4,0,(0,-3)), (0,0,3),
        (0,-2,2,(0,1)), (0,-2,-3), (0,-2,-2), (0,2,2,(-1,0)), (0,2,-3,(0,-1),(1,0)), (0,2,-2), (0,4,1,(0,1)),
        (0,4,-1), (0,-2,3,(0,1)), (0,4,3), (0,4,-3), (0,2,4), (0,4,2), (0,4,-2), (0,4,4), (0,-2,4),
    ),
    (0, False): (
        (0,-1,0,(-2,0),(0,-1),(0,-3),(0,3),(-1,0),(0,1)), (0,1,0,(0,-1),(0,1)), (0,-1,-1,(0,-1),(-1,0),(1,0)),
        (0,-1,1), (0,-3,0,(0,3),(0,-1),(-1,0)), (0,-1,3), (0,-1,-3,(-1,0)), (0,3,0,(0,-1)), (0,1,1), (0,1,-1),
        (0,-1,-2,(-1,0)), (0,1,-3,(0,-1),(1,0)), (0,-3,1,(-1,0)), (0,-3,-1,(0,-1),(-1,0)), (0,-1,2),
        (0,-3,3,(0,1),(0,-1),(-1,0)), (0,3,-1,(0,-1)), (0,3,1,(0,1)), (0,3,3,(0,1)), (0,1,3), (0,1,4,(3,0)),
        (0,-1,4), (0,-3,-2,(-1,0)), (0,1,-2), (0,-3,4,(0,1)), (0,-3,2), (0,3,-2), (0,3,2), (0,1,2), (0,3,4),
        (0,3,-3), (0,-3,-3),
    ),
    (1, True): (
        (1,0,1,(0,2),(1,0),(3,0),(-1,0)), (1,0,-2,(0,-1),(2,0),(-1,0),(1,0)), (1,0,-1,(-1,0),(1,0)),
        (1,-2,0,(0,1),(0,-2),(0,-1)), (1,0,3,(0,1),(1,0),(-2,0),(-1,0)), (1,0,2),
        (1,0,-3,(1,0),(-2,0),(-1,0)), (1,4,0,(0,2)), (1,2,0), (1,2,-2,(0,-2),(0,-1)), (1,2,1,(0,1)),
        (1,-2,1,(-1,0)), (1,-2,-2), (1,-2,-1), (1,2,-1), (1,0,4,(-3,0),(1,0)), (1,4,1,(0,2)),
        (1,-2,3,(-1,0),(0,1)), (1,-2,-3,(-1,0)), (1,4,2), (1,2,-3), (1,-2,2), (1,2,4,(1,0)), (1,2,2,(1,0)),
        (1,2,3,(1,0)), (1,4,-2,(0,1)), (1,-2,4), (1,4,3), (1,4,-3), (1,4,-1), (1,4,4),
    ),
    (1, False): (
        (1,-1,0,(-2,0)), (1,3,0,(0,-1),(1,0),(-1,0)), (1,1,0), (1,1,1,(1,0),(0,1)), (1,-1,1,(0,1)),
        (1,3,-1,(0,-1),(-1,0)), (1,3,1,(1,0)), (1,-1,-2,(0,-2)), (1,-3,0,(0,-1),(0,2)), (1,1,-2), (1,1,2),
        (1,-1,-1), (1,-1,2,(-1,0)), (1,1,-1), (1,1,3,(1,0)), (1,3,-2,(1,0),(0,-1)), (1,-1,3), (1,1,-3,(3,0)),
        (1,-1,-3), (1,-1,4), (1,-3,-1,(0,-1)), (1,-3,2), (1,-3,1), (1,3,-3), (1,1,4), (1,-3,4,(-1,0)),
        (1,-3,3), (1,-3,-3), (1,-3,-2), (1,3,2), (1,3,3), (1,3,4),
    ),
}
PIECE = TILE // PARTS


def at(x, y, z, k):
    return ((z * NY + y) * 2 + k, x)


def start(src, dst, send_sem, recv_sem, device):
    pltpu.make_async_remote_copy(
        src_ref=src, dst_ref=dst, send_sem=send_sem, recv_sem=recv_sem,
        device_id=device, device_id_type=MESH,
    ).start()


def wait(ref, sem):
    pltpu.make_async_copy(ref, ref, sem).wait()


def loop(low, high, body):
    def step(index, carry):
        body(index)
        return carry

    lax.fori_loop(low, high, step, 0)


class Place:
    def __init__(self):
        rows = lax.axis_index("rows")
        self.x = lax.axis_index("rep")
        self.k = rows % 2
        self.y = (rows // 2) % NY
        self.z = rows // (2 * NY)
        self.owner = self.x % 2
        self.on_row = self.y % 2 == self.x // 2
        self.source = self.on_row & (self.k == self.owner)
        self.panel = self.z * NS + self.y // 2


class Gather:
    def __init__(self, me, pan, recv, sent, pair):
        self.me, self.pan, self.recv, self.sent, self.pair = me, pan, recv, sent, pair

    def piece(self, p, panel):
        return self.pan.at[(p % 2) * HALF + panel, pl.ds((p // 2) * PIECE, PIECE)]

    def send(self, p, panel, dy, dz):
        ref = self.piece(p, panel)
        device = at(self.me.x, (self.me.y + dy + NY) % NY, (self.me.z + dz + NZ) % NZ, p % 2)
        start(ref, ref, self.sent, self.recv.at[p * HALF + panel], device)

    def begin(self):
        me, pan = self.me, self.pan

        @pl.when(me.source)
        def _():
            sign = 1 - 2 * (me.z % 2)
            for turn in range(max(len(moves) for moves in ROOT)):
                for p, moves in enumerate(ROOT):
                    if turn < len(moves):
                        dy, dz = moves[turn]
                        self.send(p, me.panel, sign * dy, sign * dz)
            for half in range(2):
                ref = pan.at[half * HALF + me.panel]
                start(ref, ref, self.sent, self.pair, at(me.x, me.y, me.z, 1 - me.k))

    def forward(self, low, high):
        me = self.me
        for (core, on_row), steps in STEPS.items():
            part = steps[round(low * len(steps)):round(high * len(steps))]

            @pl.when((me.k == core) & (me.on_row == on_row))
            def _(part=part):
                for p, dy, dz, *moves in part:
                    sign = 1 - 2 * ((me.z + dz) % 2)
                    z = (me.z - sign * dz + NZ) % NZ
                    y = (me.y - sign * dy + NY) % NY
                    panel = z * NS + y // 2
                    ref = self.piece(p, panel)
                    wait(ref, self.recv.at[p * HALF + panel])
                    for my, mz in moves:
                        self.send(p, panel, sign * my, sign * mz)
                    start(ref, ref, self.sent, self.pair, at(me.x, me.y, me.z, 1 - me.k))

    def finish(self):
        me = self.me

        @pl.when(me.source)
        def _():
            wait(self.pan.at[pl.ds(0, HALF - 1)], self.pair)

        @pl.when(me.on_row & jnp.logical_not(me.source))
        def _():
            wait(self.pan.at[pl.ds(0, HALF + 1)], self.pair)

        @pl.when(jnp.logical_not(me.on_row))
        def _():
            wait(self.pan.at[pl.ds(0, HALF)], self.pair)

    def end(self):
        me = self.me
        count = jnp.where(me.source, sum(len(moves) for moves in ROOT) + 2 * PARTS, 0)
        for (core, on_row), steps in STEPS.items():
            total = sum(len(step) - 2 for step in steps)
            count = count + jnp.where((me.k == core) & (me.on_row == on_row), total, 0)
        bulk = HALF * PARTS
        loop(0, count // bulk, lambda i: wait(self.pan.at[pl.ds(0, HALF)], self.sent))
        loop(0, count % bulk, lambda i: wait(self.piece(0, 0), self.sent))


def aggregate(coords, lhs, pan, rhs):
    def pick(i):
        column = coords[0, 0, 1, i]
        slot = (column % 2) * HALF + column // 8
        rhs[pl.ds(pl.multiple_of(i * TILE, TILE), TILE), :] = pan[slot]

    loop(0, KMAX, pick)
    return jnp.dot(lhs[...], rhs[...], preferred_element_type=F32)


def kernel(features, weight_in, cotangent_in, coords_in, tiles_in, act_ref, grad_ref, wg_ref,
           coords, pan1, pan2, weight, cotangent, tiles, lhs, rhs, hx, hid, slope_ref,
           wgp, wy, wz, wall, bp, bx, ig,
           f_sem, w_sem, c_sem, t_sem, i_sem, recv1, recv2, sent1, sent2, pair1, pair2, hx_recv, hx_sent, hid_recv,
           wy_recv, wz_recv, wq_recv, wx_recv, w_sent, wx_sent, bx_recv, ig_recv, b_sent):
    me = Place()
    x, y, z, k = me.x, me.y, me.z, me.k

    own = [
        pltpu.make_async_copy(features.at[pl.ds(half * TILE, TILE)],
                              pan1.at[half * HALF + me.panel], f_sem.at[half])
        for half in range(2)
    ]

    @pl.when(me.source)
    def _():
        own[0].start()
        own[1].start()

    coords_copy = pltpu.make_async_copy(coords_in, coords, i_sem)
    coords_copy.start()
    tiles_copy = pltpu.make_async_copy(tiles_in.at[0, 0], tiles, t_sem)
    tiles_copy.start()
    weight_copy = pltpu.make_async_copy(weight_in, weight, w_sem)
    weight_copy.start()
    cotangent_copy = pltpu.make_async_copy(cotangent_in, cotangent, c_sem)
    cotangent_copy.start()

    barrier = pltpu.get_barrier_semaphore()

    def hello(d):
        for core in range(2):
            pl.semaphore_signal(barrier, inc=1, device_id=at(x, (y + d) % NY, z, core),
                                device_id_type=MESH)
            pl.semaphore_signal(barrier, inc=1, device_id=at(x, y, (z + d) % NZ, core),
                                device_id_type=MESH)

    loop(1, NY, hello)
    for d in range(1, NX):
        pl.semaphore_signal(barrier, inc=1, device_id=at((x + d) % NX, y, z, k),
                            device_id_type=MESH)
    pl.semaphore_signal(barrier, inc=1, device_id=at(x, y, z, 1 - k), device_id_type=MESH)

    @pl.when(me.source)
    def _():
        own[0].wait()
        own[1].wait()

    pl.semaphore_wait(barrier, 4 * (NY - 1) + NX)

    one = Gather(me, pan1, recv1, sent1, pair1)
    two = Gather(me, pan2, recv2, sent2, pair2)
    one.begin()

    coords_copy.wait()
    tiles_copy.wait()

    def lay(i):
        row = coords[0, 0, 0, i]
        tile = tiles[i]
        columns = pl.ds(pl.multiple_of(i * TILE, TILE), TILE)
        zero = jnp.zeros_like(tile)
        lhs[0:TILE, columns] = jnp.where(row == 0, tile, zero)
        lhs[TILE:, columns] = jnp.where(row == 0, zero, tile)

    loop(0, KMAX, lay)
    weight_copy.wait()
    cotangent_copy.wait()

    one.forward(0, 1)
    one.finish()
    hx[x] = aggregate(coords, lhs, pan1, rhs).astype(BF)

    home = 2 * (y % 2) + k

    @pl.when(home != x)
    def _():
        start(hx.at[x], hx.at[x], hx_sent, hx_recv.at[x], at(home, y, z, k))

    def middle():
        v = jnp.dot(hid[...], weight[...], preferred_element_type=F32)
        s = 1.0 / (1.0 + jnp.exp(-v))
        slope_ref[...] = (cotangent[...].astype(F32) * (s * (1.0 + v * (1.0 - s)))).astype(BF)
        act_ref[...] = (v * s).astype(BF)

    @pl.when(me.source)
    def _():
        def take(d):
            wait(hx.at[(x + d) % NX], hx_recv.at[(x + d) % NX])

        loop(1, NX, take)
        hidden = (hx[0].astype(F32) + hx[1].astype(F32)) + (hx[2].astype(F32) + hx[3].astype(F32))
        hid[...] = hidden.astype(BF)
        middle()
        pan2[me.panel] = slope_ref[0:TILE, :]
        pan2[HALF + me.panel] = slope_ref[TILE:, :]

    two.begin()

    @pl.when(me.source)
    def _():
        def tell(d):
            start(hid, hid, hx_sent, hid_recv, at((x + d) % NX, y, z, k))

        loop(1, NX, tell)

    two.forward(0, CUTS[0])

    @pl.when(jnp.logical_not(me.source))
    def _():
        wait(hid, hid_recv)
        middle()

    term = lax.dot_general(hid[...], slope_ref[...], (((0,), (0,)), ((), ())),
                           preferred_element_type=F32)
    wgp[0] = term[:, 0:TILE]
    wgp[1] = term[:, TILE:]
    mine = y * 2 + k

    def chunk(to):
        return wgp.at[to % 2, pl.ds(pl.multiple_of(x * 64 + (to // 2) * 8, 8), 8), :]

    def scatter_y(d):
        to = (mine + d) % 16
        start(chunk(to), wy.at[mine], w_sent, wy_recv.at[mine], at(x, to // 2, z, to % 2))

    loop(1, 16, scatter_y)
    wy[mine] = chunk(mine)[...]

    two.forward(CUTS[0], CUTS[1])

    def take_y(d):
        src = (mine + d) % 16
        wait(wy.at[src], wy_recv.at[src])

    loop(1, 16, take_y)
    wz[z] = jnp.sum(wy[...], axis=0)

    def scatter_z(d):
        start(wz.at[z], wz.at[z], w_sent, wz_recv.at[z], at(x, y, (z + d) % NZ, k))

    loop(1, NZ, scatter_z)

    two.forward(CUTS[1], CUTS[2])

    def take_z(d):
        src = (z + d) % NZ
        wait(wz.at[src], wz_recv.at[src])

    loop(1, NZ, take_z)
    wall[x, mine] = jnp.sum(wz[...], axis=0) * (1.0 / math.sqrt(ROWS * NY * NZ * 2))

    def spread_y(d):
        to = (mine + d) % 16
        start(wall.at[x, mine], wall.at[x, mine], w_sent, wq_recv.at[mine],
              at(x, to // 2, z, to % 2))

    loop(1, 16, spread_y)

    two.forward(CUTS[2], 1)
    two.finish()

    bp[...] = aggregate(coords, lhs, pan2, rhs).astype(BF).reshape(NX, 64, F)

    def give_back(d):
        to = (x + d) % NX
        start(bp.at[to], bx.at[x], b_sent, bx_recv.at[x], at(to, y, z, k))

    loop(1, NX, give_back)
    bx[x] = bp[x]

    def take_q(d):
        src = (mine + d) % 16
        wait(wall.at[x, src], wq_recv.at[src])

    loop(1, 16, take_q)

    def spread_x(d):
        start(wall.at[x], wall.at[x], wx_sent, wx_recv.at[x], at((x + d) % NX, y, z, k))

    loop(1, NX, spread_x)

    def take_back(d):
        wait(bx.at[(x + d) % NX], bx_recv.at[(x + d) % NX])

    loop(1, NX, take_back)
    total = (bx[0].astype(F32) + bx[1].astype(F32)) + (bx[2].astype(F32) + bx[3].astype(F32))
    ig[x] = lax.dot_general(total.astype(BF), weight[...], (((1,), (1,)), ((), ())),
                            preferred_element_type=F32).astype(BF)

    def give_grad(d):
        start(ig.at[x], ig.at[x], b_sent, ig_recv.at[x], at((x + d) % NX, y, z, k))

    loop(1, NX, give_grad)

    one.end()
    two.end()
    loop(0, jnp.where(me.source, NX - 1, 1), lambda d: wait(hx.at[0], hx_sent))
    loop(0, 15 + 7 + 15, lambda i: wait(wz.at[0], w_sent))

    def take_x(d):
        wait(wall.at[(x + d) % NX], wx_recv.at[(x + d) % NX])

    loop(1, NX, take_x)
    for quarter in range(NX):
        for row in range(8):
            for half in range(2):
                wg_ref[quarter * 64 + row * 8:quarter * 64 + row * 8 + 8,
                       half * TILE:(half + 1) * TILE] = wall[quarter, row * 2 + half]

    def take_grad(d):
        wait(ig.at[(x + d) % NX], ig_recv.at[(x + d) % NX])

    loop(1, NX, take_grad)
    grad_ref[...] = ig[...].reshape(ROWS, F)
    loop(1, NX, lambda d: wait(wall.at[0], wx_sent))
    loop(0, 6, lambda i: wait(bp.at[0], b_sent))


CUTS = (0.3, 0.55, 0.8)


def write_out(act, grad, wg, act_out, grad_out, wg_out, sems):
    copies = [
        pltpu.make_async_copy(src, dst, sems.at[i])
        for i, (src, dst) in enumerate(((act, act_out), (grad, grad_out), (wg, wg_out)))
    ]
    for copy in copies:
        copy.start()
    for copy in copies:
        copy.wait()


def pin(value):
    return pltpu.with_memory_space_constraint(value, pltpu.HBM)


def on_device(features, weight, cotangent, tile_coords, tile_count, tiles):
    vmem = pl.BlockSpec(memory_space=pltpu.VMEM)
    hbm = pl.BlockSpec(memory_space=pltpu.HBM)
    dma = pltpu.SemaphoreType.DMA
    shapes = (
        jax.ShapeDtypeStruct((ROWS, F), BF),
        jax.ShapeDtypeStruct((ROWS, F), BF),
        jax.ShapeDtypeStruct((F, F), F32),
    )
    results = pl.pallas_call(
        kernel,
        out_shape=(pltpu.VMEM((ROWS, F), BF), pltpu.VMEM((ROWS, F), BF), pltpu.VMEM((F, F), F32)),
        in_specs=[hbm, hbm, hbm, hbm, hbm],
        out_specs=(vmem, vmem, vmem),
        scratch_shapes=[
            pltpu.SMEM((1, 1, 2, KMAX), jnp.int32),
            pltpu.VMEM((2 * HALF, TILE, F), BF),
            pltpu.VMEM((2 * HALF, TILE, F), BF),
            pltpu.VMEM((F, F), BF),
            pltpu.VMEM((ROWS, F), BF),
            pltpu.VMEM((KMAX, TILE, TILE), BF),
            pltpu.VMEM((2 * TILE, KMAX * TILE), BF),
            pltpu.VMEM((KMAX * TILE, F), BF),
            pltpu.VMEM((NX, ROWS, F), BF),
            pltpu.VMEM((ROWS, F), BF),
            pltpu.VMEM((ROWS, F), BF),
            pltpu.VMEM((2, F, TILE), F32),
            pltpu.VMEM((16, 8, TILE), F32),
            pltpu.VMEM((NZ, 8, TILE), F32),
            pltpu.VMEM((NX, 16, 8, TILE), F32),
            pltpu.VMEM((NX, 64, F), BF),
            pltpu.VMEM((NX, 64, F), BF),
            pltpu.VMEM((NX, 64, F), BF),
            dma((2,)), dma(()), dma(()), dma(()), dma(()),
            dma((2 * PARTS * HALF,)), dma((2 * PARTS * HALF,)), dma(()), dma(()), dma(()), dma(()),
            dma((NX,)), dma(()), dma(()),
            dma((16,)), dma((NZ,)), dma((16,)), dma((NX,)), dma(()), dma(()),
            dma((NX,)), dma((NX,)), dma(()),
        ],
        compiler_params=pltpu.CompilerParams(
            collective_id=0, has_side_effects=True, vmem_limit_bytes=24 << 20
        ),
        name="graph_layer",
    )(pin(features), pin(weight), pin(cotangent), pin(jnp.swapaxes(tile_coords, 2, 3)), pin(tiles))
    return pl.pallas_call(
        write_out,
        out_shape=shapes,
        in_specs=[vmem, vmem, vmem],
        out_specs=(hbm, hbm, hbm),
        scratch_shapes=[dma((3,))],
        compiler_params=pltpu.CompilerParams(vmem_limit_bytes=4 << 20),
        name="write_out",
    )(*[pltpu.with_memory_space_constraint(result, pltpu.VMEM) for result in results])


def solution(mesh):
    placed = (
        P("rows", None),
        P(),
        P("rows", None),
        P("rows", "rep", None, None),
        P("rows", "rep"),
        P("rows", "rep", None, None, None),
    )
    return jax.shard_map(
        on_device,
        mesh=mesh,
        in_specs=placed,
        out_specs=(P("rows", None), P("rows", None), P()),
        check_vma=False,
    )
```

```python
import math

import jax
import jax.numpy as jnp
from jax import lax
from jax.experimental import pallas as pl
from jax.experimental.pallas import tpu as pltpu
from jax.sharding import PartitionSpec as P

MESH = pl.DeviceIdType.MESH
NX, NY, NZ = 4, 8, 8
NS = NY // 2
HALF = NS * NZ
ROWS, F, TILE, KMAX = 256, 256, 128, 20
BF, F32 = jnp.bfloat16, jnp.float32

PARTS = 1
ROOT = (
    ((-1,0,1), (0,1,1), (0,-3,1), (2,0,1), (1,0,1),),
    ((0,1,1), (3,0,1), (0,-2,1), (-1,0,1), (-2,0,1), (0,-1,1), (0,2,1), (1,0,1),),
)
STEPS = {
    (0, True): (
        (0,0,1,1,(-2,0,1),(0,1,1)), (0,2,0,1,(0,3,1),(0,1,1),(1,0,1),(0,-1,1)),
        (0,0,-3,1,(1,0,1),(0,1,1),(0,-1,1)), (0,-2,0,1), (0,-2,1,1,(-1,0,1),(0,1,1)),
        (0,0,2,1,(-1,0,1),(0,1,1)), (0,2,1,1,(1,0,1)), (0,2,3,1,(0,-1,1),(1,0,1),(-1,0,1)),
        (0,2,-1,1,(0,-1,1)), (0,-2,-1,1), (0,0,4,1,(-1,0,1)), (0,0,-2,1,(1,0,1)), (0,0,-1,1),
        (0,4,0,1,(0,-3,1)), (0,0,3,1), (0,-2,2,1,(0,1,1)), (0,-2,-3,1), (0,-2,-2,1), (0,2,2,1,(-1,0,1)),
        (0,2,-3,1,(0,-1,1),(1,0,1)), (0,2,-2,1), (0,4,1,1,(0,1,1)), (0,4,-1,1), (0,-2,3,1,(0,1,1)), (0,4,3,1),
        (0,4,-3,1), (0,2,4,1), (0,4,2,1), (0,4,-2,1), (0,4,4,1), (0,-2,4,1),
    ),
    (0, False): (
        (0,-1,0,1,(-2,0,1),(0,-1,1),(0,-3,1),(0,3,1),(-1,0,1),(0,1,1)), (0,1,0,1,(0,-1,1),(0,1,1)),
        (0,-1,-1,1,(0,-1,1),(-1,0,1),(1,0,1)), (0,-1,1,1), (0,-3,0,1,(0,3,1),(0,-1,1),(-1,0,1)), (0,-1,3,1),
        (0,-1,-3,1,(-1,0,1)), (0,3,0,1,(0,-1,1)), (0,1,1,1), (0,1,-1,1), (0,-1,-2,1,(-1,0,1)),
        (0,1,-3,1,(0,-1,1),(1,0,1)), (0,-3,1,1,(-1,0,1)), (0,-3,-1,1,(0,-1,1),(-1,0,1)), (0,-1,2,1),
        (0,-3,3,1,(0,1,1),(0,-1,1),(-1,0,1)), (0,3,-1,1,(0,-1,1)), (0,3,1,1,(0,1,1)), (0,3,3,1,(0,1,1)),
        (0,1,3,1), (0,1,4,1,(3,0,1)), (0,-1,4,1), (0,-3,-2,1,(-1,0,1)), (0,1,-2,1), (0,-3,4,1,(0,1,1)),
        (0,-3,2,1), (0,3,-2,1), (0,3,2,1), (0,1,2,1), (0,3,4,1), (0,3,-3,1), (0,-3,-3,1),
    ),
    (1, True): (
        (1,0,1,1,(0,2,1),(1,0,1),(3,0,1),(-1,0,1)), (1,0,-2,1,(0,-1,1),(2,0,1),(-1,0,1),(1,0,1)),
        (1,0,-1,1,(-1,0,1),(1,0,1)), (1,-2,0,1,(0,1,1),(0,-2,1),(0,-1,1)),
        (1,0,3,1,(0,1,1),(1,0,1),(-2,0,1),(-1,0,1)), (1,0,2,1), (1,0,-3,1,(1,0,1),(-2,0,1),(-1,0,1)),
        (1,4,0,1,(0,2,1)), (1,2,0,1), (1,2,-2,1,(0,-2,1),(0,-1,1)), (1,2,1,1,(0,1,1)), (1,-2,1,1,(-1,0,1)),
        (1,-2,-2,1), (1,-2,-1,1), (1,2,-1,1), (1,0,4,1,(-3,0,1),(1,0,1)), (1,4,1,1,(0,2,1)),
        (1,-2,3,1,(-1,0,1),(0,1,1)), (1,-2,-3,1,(-1,0,1)), (1,4,2,1), (1,2,-3,1), (1,-2,2,1),
        (1,2,4,1,(1,0,1)), (1,2,2,1,(1,0,1)), (1,2,3,1,(1,0,1)), (1,4,-2,1,(0,1,1)), (1,-2,4,1), (1,4,3,1),
        (1,4,-3,1), (1,4,-1,1), (1,4,4,1),
    ),
    (1, False): (
        (1,-1,0,1,(-2,0,1)), (1,3,0,1,(0,-1,1),(1,0,1),(-1,0,1)), (1,1,0,1), (1,1,1,1,(1,0,1),(0,1,1)),
        (1,-1,1,1,(0,1,1)), (1,3,-1,1,(0,-1,1),(-1,0,1)), (1,3,1,1,(1,0,1)), (1,-1,-2,1,(0,-2,1)),
        (1,-3,0,1,(0,-1,1),(0,2,1)), (1,1,-2,1), (1,1,2,1), (1,-1,-1,1), (1,-1,2,1,(-1,0,1)), (1,1,-1,1),
        (1,1,3,1,(1,0,1)), (1,3,-2,1,(1,0,1),(0,-1,1)), (1,-1,3,1), (1,1,-3,1,(3,0,1)), (1,-1,-3,1),
        (1,-1,4,1), (1,-3,-1,1,(0,-1,1)), (1,-3,2,1), (1,-3,1,1), (1,3,-3,1), (1,1,4,1), (1,-3,4,1,(-1,0,1)),
        (1,-3,3,1), (1,-3,-3,1), (1,-3,-2,1), (1,3,2,1), (1,3,3,1), (1,3,4,1),
    ),
}
PIECE = TILE // PARTS


def at(x, y, z, k):
    return ((z * NY + y) * 2 + k, x)


def start(src, dst, send_sem, recv_sem, device):
    pltpu.make_async_remote_copy(
        src_ref=src, dst_ref=dst, send_sem=send_sem, recv_sem=recv_sem,
        device_id=device, device_id_type=MESH,
    ).start()


def wait(ref, sem):
    pltpu.make_async_copy(ref, ref, sem).wait()


def loop(low, high, body):
    def step(index, carry):
        body(index)
        return carry

    lax.fori_loop(low, high, step, 0)


class Place:
    def __init__(self):
        rows = lax.axis_index("rows")
        self.x = lax.axis_index("rep")
        self.k = rows % 2
        self.y = (rows // 2) % NY
        self.z = rows // (2 * NY)
        self.owner = self.x % 2
        self.on_row = self.y % 2 == self.x // 2
        self.source = self.on_row & (self.k == self.owner)
        self.panel = self.z * NS + self.y // 2


class Gather:
    def __init__(self, me, pan, recv, sent, pair):
        self.me, self.pan, self.recv, self.sent, self.pair = me, pan, recv, sent, pair

    def piece(self, p, panel):
        return self.pan.at[(p % 2) * HALF + panel, pl.ds((p // 2) * PIECE, PIECE)]

    def send(self, p, panel, sign, move):
        dy, dz, cores = move
        ref = self.piece(p, panel)
        y = (self.me.y + sign * dy + NY) % NY
        z = (self.me.z + sign * dz + NZ) % NZ
        start(ref, ref, self.sent, self.recv.at[p * HALF + panel], at(self.me.x, y, z, p % 2))
        if cores == 2:
            start(ref, ref, self.sent, self.pair, at(self.me.x, y, z, 1 - p % 2))

    def root(self, pieces):
        sign = 1 - 2 * (self.me.z % 2)
        for turn in range(max(len(ROOT[p]) for p in pieces)):
            for p in pieces:
                if turn < len(ROOT[p]):
                    self.send(p, self.me.panel, sign, ROOT[p][turn])

    def mate(self):
        me = self.me
        for half in range(2):
            ref = self.pan.at[half * HALF + me.panel]
            start(ref, ref, self.sent, self.pair, at(me.x, me.y, me.z, 1 - me.k))

    def forward(self, low, high):
        me = self.me
        for (core, on_row), steps in STEPS.items():
            part = steps[round(low * len(steps)):round(high * len(steps))]

            @pl.when((me.k == core) & (me.on_row == on_row))
            def _(part=part):
                for p, dy, dz, share, *moves in part:
                    sign = 1 - 2 * ((me.z + dz) % 2)
                    z = (me.z - sign * dz + NZ) % NZ
                    y = (me.y - sign * dy + NY) % NY
                    panel = z * NS + y // 2
                    ref = self.piece(p, panel)
                    wait(ref, self.recv.at[p * HALF + panel])
                    for move in moves:
                        self.send(p, panel, sign, move)
                    if share:
                        start(ref, ref, self.sent, self.pair, at(me.x, me.y, me.z, 1 - me.k))

    def finish(self):
        me = self.me

        @pl.when(me.source)
        def _():
            wait(self.pan.at[pl.ds(0, HALF - 1)], self.pair)

        @pl.when(me.on_row & jnp.logical_not(me.source))
        def _():
            wait(self.pan.at[pl.ds(0, HALF + 1)], self.pair)

        @pl.when(jnp.logical_not(me.on_row))
        def _():
            wait(self.pan.at[pl.ds(0, HALF)], self.pair)

    def end(self):
        me = self.me
        count = jnp.where(me.source, sum(move[2] for moves in ROOT for move in moves) + 2 * PARTS, 0)
        for (core, on_row), steps in STEPS.items():
            total = sum(step[3] + sum(move[2] for move in step[4:]) for step in steps)
            count = count + jnp.where((me.k == core) & (me.on_row == on_row), total, 0)
        bulk = HALF * PARTS
        loop(0, count // bulk, lambda i: wait(self.pan.at[pl.ds(0, HALF)], self.sent))
        loop(0, count % bulk, lambda i: wait(self.piece(0, 0), self.sent))


def aggregate(coords, lhs, pan, rhs):
    def pick(i):
        column = coords[0, 0, 1, i]
        slot = (column % 2) * HALF + column // 8
        rhs[pl.ds(pl.multiple_of(i * TILE, TILE), TILE), :] = pan[slot]

    loop(0, KMAX, pick)
    return jnp.dot(lhs[...], rhs[...], preferred_element_type=F32)


def kernel(features, weight_in, cotangent_in, coords_in, tiles_in, act_ref, grad_ref, wg_ref,
           coords, pan1, pan2, weight, cotangent, tiles, lhs, rhs, hx, hid, slope_ref,
           wgp, wy, wz, wall, bp, bx, ig,
           f_sem, w_sem, c_sem, t_sem, i_sem, recv1, recv2, sent1, sent2, pair1, pair2, hx_recv, hx_sent, hid_recv,
           wy_recv, wz_recv, wq_recv, wx_recv, w_sent, wx_sent, bx_recv, ig_recv, b_sent):
    me = Place()
    x, y, z, k = me.x, me.y, me.z, me.k

    own = [
        pltpu.make_async_copy(features.at[pl.ds(half * TILE, TILE)],
                              pan1.at[half * HALF + me.panel], f_sem.at[half])
        for half in range(2)
    ]

    @pl.when(me.source)
    def _():
        own[0].start()
        own[1].start()

    coords_copy = pltpu.make_async_copy(coords_in, coords, i_sem)
    coords_copy.start()
    tiles_copy = pltpu.make_async_copy(tiles_in.at[0, 0], tiles, t_sem)
    tiles_copy.start()
    weight_copy = pltpu.make_async_copy(weight_in, weight, w_sem)
    weight_copy.start()
    cotangent_copy = pltpu.make_async_copy(cotangent_in, cotangent, c_sem)
    cotangent_copy.start()

    barrier = pltpu.get_barrier_semaphore()

    def hello(d):
        for core in range(2):
            pl.semaphore_signal(barrier, inc=1, device_id=at(x, (y + d) % NY, z, core),
                                device_id_type=MESH)
            pl.semaphore_signal(barrier, inc=1, device_id=at(x, y, (z + d) % NZ, core),
                                device_id_type=MESH)

    loop(1, NY, hello)
    for d in range(1, NX):
        pl.semaphore_signal(barrier, inc=1, device_id=at((x + d) % NX, y, z, k),
                            device_id_type=MESH)
    pl.semaphore_signal(barrier, inc=1, device_id=at(x, y, z, 1 - k), device_id_type=MESH)

    @pl.when(me.source)
    def _():
        own[0].wait()
        own[1].wait()

    pl.semaphore_wait(barrier, 4 * (NY - 1) + NX)

    one = Gather(me, pan1, recv1, sent1, pair1)
    two = Gather(me, pan2, recv2, sent2, pair2)

    @pl.when(me.source)
    def _():
        one.root(range(2 * PARTS))
        one.mate()

    coords_copy.wait()
    tiles_copy.wait()

    def lay(i):
        row = coords[0, 0, 0, i]
        tile = tiles[i]
        columns = pl.ds(pl.multiple_of(i * TILE, TILE), TILE)
        zero = jnp.zeros_like(tile)
        lhs[0:TILE, columns] = jnp.where(row == 0, tile, zero)
        lhs[TILE:, columns] = jnp.where(row == 0, zero, tile)

    loop(0, KMAX, lay)
    weight_copy.wait()
    cotangent_copy.wait()

    one.forward(0, 1)
    one.finish()
    partial = aggregate(coords, lhs, pan1, rhs)

    home = 2 * (y % 2) + k
    halves = [pl.ds(half * TILE, TILE) for half in range(2)]
    for half, rows in enumerate(halves):
        hx[x, rows, :] = partial[half * TILE:(half + 1) * TILE, :].astype(BF)

        @pl.when(home != x)
        def _(half=half, rows=rows):
            start(hx.at[x, rows], hx.at[x, rows], hx_sent, hx_recv.at[half * NX + x],
                  at(home, y, z, k))

    def middle(rows):
        v = jnp.dot(hid[rows, :], weight[...], preferred_element_type=F32)
        s = 1.0 / (1.0 + jnp.exp(-v))
        slope = cotangent[rows, :].astype(F32) * (s * (1.0 + v * (1.0 - s)))
        slope_ref[rows, :] = slope.astype(BF)
        act_ref[rows, :] = (v * s).astype(BF)

    @pl.when(me.source)
    def _():
        for half, rows in enumerate(halves):
            def take(d, half=half, rows=rows):
                other = (x + d) % NX
                wait(hx.at[other, rows], hx_recv.at[half * NX + other])

            loop(1, NX, take)
            terms = [hx[j, rows, :].astype(F32) for j in range(NX)]
            hid[rows, :] = ((terms[0] + terms[1]) + (terms[2] + terms[3])).astype(BF)
            middle(rows)
            pan2[half * HALF + me.panel] = slope_ref[rows, :]
            two.root(range(half, 2 * PARTS, 2))
        two.mate()

        def tell(d):
            start(hid, hid, hx_sent, hid_recv, at((x + d) % NX, y, z, k))

        loop(1, NX, tell)

    two.forward(0, CUTS[0])

    @pl.when(jnp.logical_not(me.source))
    def _():
        wait(hid, hid_recv)
        for rows in halves:
            middle(rows)

    term = lax.dot_general(hid[...], slope_ref[...], (((0,), (0,)), ((), ())),
                           preferred_element_type=F32)
    wgp[0] = term[:, 0:TILE]
    wgp[1] = term[:, TILE:]
    mine = y * 2 + k

    def chunk(to):
        return wgp.at[to % 2, pl.ds(pl.multiple_of(x * 64 + (to // 2) * 8, 8), 8), :]

    def scatter_y(d):
        to = (mine + d) % 16
        start(chunk(to), wy.at[mine], w_sent, wy_recv.at[mine], at(x, to // 2, z, to % 2))

    loop(1, 16, scatter_y)
    wy[mine] = chunk(mine)[...]

    two.forward(CUTS[0], CUTS[1])

    def take_y(d):
        src = (mine + d) % 16
        wait(wy.at[src], wy_recv.at[src])

    loop(1, 16, take_y)
    wz[z] = jnp.sum(wy[...], axis=0)

    def scatter_z(d):
        start(wz.at[z], wz.at[z], w_sent, wz_recv.at[z], at(x, y, (z + d) % NZ, k))

    loop(1, NZ, scatter_z)

    two.forward(CUTS[1], CUTS[2])

    def take_z(d):
        src = (z + d) % NZ
        wait(wz.at[src], wz_recv.at[src])

    loop(1, NZ, take_z)
    wall[x, mine] = jnp.sum(wz[...], axis=0) * (1.0 / math.sqrt(ROWS * NY * NZ * 2))

    def spread_y(d):
        to = (mine + d) % 16
        start(wall.at[x, mine], wall.at[x, mine], w_sent, wq_recv.at[mine],
              at(x, to // 2, z, to % 2))

    loop(1, 16, spread_y)

    two.forward(CUTS[2], 1)
    two.finish()

    bp[...] = aggregate(coords, lhs, pan2, rhs).astype(BF).reshape(NX, 64, F)

    def give_back(d):
        to = (x + d) % NX
        start(bp.at[to], bx.at[x], b_sent, bx_recv.at[x], at(to, y, z, k))

    loop(1, NX, give_back)
    bx[x] = bp[x]

    def take_q(d):
        src = (mine + d) % 16
        wait(wall.at[x, src], wq_recv.at[src])

    loop(1, 16, take_q)

    def spread_x(d):
        start(wall.at[x], wall.at[x], wx_sent, wx_recv.at[x], at((x + d) % NX, y, z, k))

    loop(1, NX, spread_x)

    def take_back(d):
        wait(bx.at[(x + d) % NX], bx_recv.at[(x + d) % NX])

    loop(1, NX, take_back)
    total = (bx[0].astype(F32) + bx[1].astype(F32)) + (bx[2].astype(F32) + bx[3].astype(F32))
    ig[x] = lax.dot_general(total.astype(BF), weight[...], (((1,), (1,)), ((), ())),
                            preferred_element_type=F32).astype(BF)

    def give_grad(d):
        start(ig.at[x], ig.at[x], b_sent, ig_recv.at[x], at((x + d) % NX, y, z, k))

    loop(1, NX, give_grad)

    one.end()
    two.end()
    loop(0, jnp.where(me.source, NX - 1, 1), lambda d: wait(hx.at[0], hx_sent))
    loop(0, 15 + 7 + 15, lambda i: wait(wz.at[0], w_sent))

    def take_x(d):
        wait(wall.at[(x + d) % NX], wx_recv.at[(x + d) % NX])

    loop(1, NX, take_x)
    for quarter in range(NX):
        for row in range(8):
            for half in range(2):
                wg_ref[quarter * 64 + row * 8:quarter * 64 + row * 8 + 8,
                       half * TILE:(half + 1) * TILE] = wall[quarter, row * 2 + half]

    def take_grad(d):
        wait(ig.at[(x + d) % NX], ig_recv.at[(x + d) % NX])

    loop(1, NX, take_grad)
    grad_ref[...] = ig[...].reshape(ROWS, F)
    loop(1, NX, lambda d: wait(wall.at[0], wx_sent))
    loop(0, 6, lambda i: wait(bp.at[0], b_sent))


CUTS = (0.2, 0.5, 0.8)


def write_out(act, grad, wg, act_out, grad_out, wg_out, sems):
    copies = [
        pltpu.make_async_copy(src, dst, sems.at[i])
        for i, (src, dst) in enumerate(((act, act_out), (grad, grad_out), (wg, wg_out)))
    ]
    for copy in copies:
        copy.start()
    for copy in copies:
        copy.wait()


def pin(value):
    return pltpu.with_memory_space_constraint(value, pltpu.HBM)


def on_device(features, weight, cotangent, tile_coords, tile_count, tiles):
    vmem = pl.BlockSpec(memory_space=pltpu.VMEM)
    hbm = pl.BlockSpec(memory_space=pltpu.HBM)
    dma = pltpu.SemaphoreType.DMA
    shapes = (
        jax.ShapeDtypeStruct((ROWS, F), BF),
        jax.ShapeDtypeStruct((ROWS, F), BF),
        jax.ShapeDtypeStruct((F, F), F32),
    )
    results = pl.pallas_call(
        kernel,
        out_shape=(pltpu.VMEM((ROWS, F), BF), pltpu.VMEM((ROWS, F), BF), pltpu.VMEM((F, F), F32)),
        in_specs=[hbm, hbm, hbm, hbm, hbm],
        out_specs=(vmem, vmem, vmem),
        scratch_shapes=[
            pltpu.SMEM((1, 1, 2, KMAX), jnp.int32),
            pltpu.VMEM((2 * HALF, TILE, F), BF),
            pltpu.VMEM((2 * HALF, TILE, F), BF),
            pltpu.VMEM((F, F), BF),
            pltpu.VMEM((ROWS, F), BF),
            pltpu.VMEM((KMAX, TILE, TILE), BF),
            pltpu.VMEM((2 * TILE, KMAX * TILE), BF),
            pltpu.VMEM((KMAX * TILE, F), BF),
            pltpu.VMEM((NX, ROWS, F), BF),
            pltpu.VMEM((ROWS, F), BF),
            pltpu.VMEM((ROWS, F), BF),
            pltpu.VMEM((2, F, TILE), F32),
            pltpu.VMEM((16, 8, TILE), F32),
            pltpu.VMEM((NZ, 8, TILE), F32),
            pltpu.VMEM((NX, 16, 8, TILE), F32),
            pltpu.VMEM((NX, 64, F), BF),
            pltpu.VMEM((NX, 64, F), BF),
            pltpu.VMEM((NX, 64, F), BF),
            dma((2,)), dma(()), dma(()), dma(()), dma(()),
            dma((2 * PARTS * HALF,)), dma((2 * PARTS * HALF,)), dma(()), dma(()), dma(()), dma(()),
            dma((2 * NX,)), dma(()), dma(()),
            dma((16,)), dma((NZ,)), dma((16,)), dma((NX,)), dma(()), dma(()),
            dma((NX,)), dma((NX,)), dma(()),
        ],
        compiler_params=pltpu.CompilerParams(
            collective_id=0, has_side_effects=True, vmem_limit_bytes=24 << 20
        ),
        name="graph_layer",
    )(pin(features), pin(weight), pin(cotangent), pin(jnp.swapaxes(tile_coords, 2, 3)), pin(tiles))
    return pl.pallas_call(
        write_out,
        out_shape=shapes,
        in_specs=[vmem, vmem, vmem],
        out_specs=(hbm, hbm, hbm),
        scratch_shapes=[dma((3,))],
        compiler_params=pltpu.CompilerParams(vmem_limit_bytes=4 << 20),
        name="write_out",
    )(*[pltpu.with_memory_space_constraint(result, pltpu.VMEM) for result in results])


def solution(mesh):
    placed = (
        P("rows", None),
        P(),
        P("rows", None),
        P("rows", "rep", None, None),
        P("rows", "rep"),
        P("rows", "rep", None, None, None),
    )
    return jax.shard_map(
        on_device,
        mesh=mesh,
        in_specs=placed,
        out_specs=(P("rows", None), P("rows", None), P()),
        check_vma=False,
    )
```

```python
import math

import jax
import jax.numpy as jnp
from jax import lax
from jax.experimental import pallas as pl
from jax.experimental.pallas import tpu as pltpu
from jax.sharding import PartitionSpec as P

MESH = pl.DeviceIdType.MESH
NX, NY, NZ = 4, 8, 8
NS = NY // 2
HALF = NS * NZ
ROWS, F, TILE, KMAX = 256, 256, 128, 20
BF, F32 = jnp.bfloat16, jnp.float32

PARTS = 1
ROOT = (
    ((-1,0,1), (0,1,1), (0,-3,1), (2,0,1), (1,0,1),),
    ((0,1,1), (3,0,1), (0,-2,1), (-1,0,1), (-2,0,1), (0,-1,1), (0,2,1), (1,0,1),),
)
STEPS = {
    (0, True): (
        (0,0,1,1,(-2,0,1),(0,1,1)), (0,2,0,1,(0,3,1),(0,1,1),(1,0,1),(0,-1,1)),
        (0,0,-3,1,(1,0,1),(0,1,1),(0,-1,1)), (0,-2,0,1), (0,-2,1,1,(-1,0,1),(0,1,1)),
        (0,0,2,1,(-1,0,1),(0,1,1)), (0,2,1,1,(1,0,1)), (0,2,3,1,(0,-1,1),(1,0,1),(-1,0,1)),
        (0,2,-1,1,(0,-1,1)), (0,-2,-1,1), (0,0,4,1,(-1,0,1)), (0,0,-2,1,(1,0,1)), (0,0,-1,1),
        (0,4,0,1,(0,-3,1)), (0,0,3,1), (0,-2,2,1,(0,1,1)), (0,-2,-3,1), (0,-2,-2,1), (0,2,2,1,(-1,0,1)),
        (0,2,-3,1,(0,-1,1),(1,0,1)), (0,2,-2,1), (0,4,1,1,(0,1,1)), (0,4,-1,1), (0,-2,3,1,(0,1,1)), (0,4,3,1),
        (0,4,-3,1), (0,2,4,1), (0,4,2,1), (0,4,-2,1), (0,4,4,1), (0,-2,4,1),
    ),
    (0, False): (
        (0,-1,0,1,(-2,0,1),(0,-1,1),(0,-3,1),(0,3,1),(-1,0,1),(0,1,1)), (0,1,0,1,(0,-1,1),(0,1,1)),
        (0,-1,-1,1,(0,-1,1),(-1,0,1),(1,0,1)), (0,-1,1,1), (0,-3,0,1,(0,3,1),(0,-1,1),(-1,0,1)), (0,-1,3,1),
        (0,-1,-3,1,(-1,0,1)), (0,3,0,1,(0,-1,1)), (0,1,1,1), (0,1,-1,1), (0,-1,-2,1,(-1,0,1)),
        (0,1,-3,1,(0,-1,1),(1,0,1)), (0,-3,1,1,(-1,0,1)), (0,-3,-1,1,(0,-1,1),(-1,0,1)), (0,-1,2,1),
        (0,-3,3,1,(0,1,1),(0,-1,1),(-1,0,1)), (0,3,-1,1,(0,-1,1)), (0,3,1,1,(0,1,1)), (0,3,3,1,(0,1,1)),
        (0,1,3,1), (0,1,4,1,(3,0,1)), (0,-1,4,1), (0,-3,-2,1,(-1,0,1)), (0,1,-2,1), (0,-3,4,1,(0,1,1)),
        (0,-3,2,1), (0,3,-2,1), (0,3,2,1), (0,1,2,1), (0,3,4,1), (0,3,-3,1), (0,-3,-3,1),
    ),
    (1, True): (
        (1,0,1,1,(0,2,1),(1,0,1),(3,0,1),(-1,0,1)), (1,0,-2,1,(0,-1,1),(2,0,1),(-1,0,1),(1,0,1)),
        (1,0,-1,1,(-1,0,1),(1,0,1)), (1,-2,0,1,(0,1,1),(0,-2,1),(0,-1,1)),
        (1,0,3,1,(0,1,1),(1,0,1),(-2,0,1),(-1,0,1)), (1,0,2,1), (1,0,-3,1,(1,0,1),(-2,0,1),(-1,0,1)),
        (1,4,0,1,(0,2,1)), (1,2,0,1), (1,2,-2,1,(0,-2,1),(0,-1,1)), (1,2,1,1,(0,1,1)), (1,-2,1,1,(-1,0,1)),
        (1,-2,-2,1), (1,-2,-1,1), (1,2,-1,1), (1,0,4,1,(-3,0,1),(1,0,1)), (1,4,1,1,(0,2,1)),
        (1,-2,3,1,(-1,0,1),(0,1,1)), (1,-2,-3,1,(-1,0,1)), (1,4,2,1), (1,2,-3,1), (1,-2,2,1),
        (1,2,4,1,(1,0,1)), (1,2,2,1,(1,0,1)), (1,2,3,1,(1,0,1)), (1,4,-2,1,(0,1,1)), (1,-2,4,1), (1,4,3,1),
        (1,4,-3,1), (1,4,-1,1), (1,4,4,1),
    ),
    (1, False): (
        (1,-1,0,1,(-2,0,1)), (1,3,0,1,(0,-1,1),(1,0,1),(-1,0,1)), (1,1,0,1), (1,1,1,1,(1,0,1),(0,1,1)),
        (1,-1,1,1,(0,1,1)), (1,3,-1,1,(0,-1,1),(-1,0,1)), (1,3,1,1,(1,0,1)), (1,-1,-2,1,(0,-2,1)),
        (1,-3,0,1,(0,-1,1),(0,2,1)), (1,1,-2,1), (1,1,2,1), (1,-1,-1,1), (1,-1,2,1,(-1,0,1)), (1,1,-1,1),
        (1,1,3,1,(1,0,1)), (1,3,-2,1,(1,0,1),(0,-1,1)), (1,-1,3,1), (1,1,-3,1,(3,0,1)), (1,-1,-3,1),
        (1,-1,4,1), (1,-3,-1,1,(0,-1,1)), (1,-3,2,1), (1,-3,1,1), (1,3,-3,1), (1,1,4,1), (1,-3,4,1,(-1,0,1)),
        (1,-3,3,1), (1,-3,-3,1), (1,-3,-2,1), (1,3,2,1), (1,3,3,1), (1,3,4,1),
    ),
}
PIECE = TILE // PARTS


def at(x, y, z, k):
    return ((z * NY + y) * 2 + k, x)


def start(src, dst, send_sem, recv_sem, device):
    pltpu.make_async_remote_copy(
        src_ref=src, dst_ref=dst, send_sem=send_sem, recv_sem=recv_sem,
        device_id=device, device_id_type=MESH,
    ).start()


def wait(ref, sem):
    pltpu.make_async_copy(ref, ref, sem).wait()


def loop(low, high, body):
    def step(index, carry):
        body(index)
        return carry

    lax.fori_loop(low, high, step, 0)


class Place:
    def __init__(self):
        rows = lax.axis_index("rows")
        self.x = lax.axis_index("rep")
        self.k = rows % 2
        self.y = (rows // 2) % NY
        self.z = rows // (2 * NY)
        self.owner = self.x % 2
        self.on_row = self.y % 2 == self.x // 2
        self.source = self.on_row & (self.k == self.owner)
        self.panel = self.z * NS + self.y // 2


class Gather:
    def __init__(self, me, pan, recv, sent, pair):
        self.me, self.pan, self.recv, self.sent, self.pair = me, pan, recv, sent, pair

    def piece(self, p, panel):
        return self.pan.at[(p % 2) * HALF + panel, pl.ds((p // 2) * PIECE, PIECE)]

    def send(self, p, panel, sign, move):
        dy, dz, cores = move
        ref = self.piece(p, panel)
        y = (self.me.y + sign * dy + NY) % NY
        z = (self.me.z + sign * dz + NZ) % NZ
        start(ref, ref, self.sent, self.recv.at[p * HALF + panel], at(self.me.x, y, z, p % 2))
        if cores == 2:
            start(ref, ref, self.sent, self.pair, at(self.me.x, y, z, 1 - p % 2))

    def root(self, pieces):
        sign = 1 - 2 * (self.me.z % 2)
        for turn in range(max(len(ROOT[p]) for p in pieces)):
            for p in pieces:
                if turn < len(ROOT[p]):
                    self.send(p, self.me.panel, sign, ROOT[p][turn])

    def mate(self):
        me = self.me
        for half in range(2):
            ref = self.pan.at[half * HALF + me.panel]
            start(ref, ref, self.sent, self.pair, at(me.x, me.y, me.z, 1 - me.k))

    def forward(self, low, high):
        me = self.me
        for (core, on_row), steps in STEPS.items():
            part = steps[round(low * len(steps)):round(high * len(steps))]

            @pl.when((me.k == core) & (me.on_row == on_row))
            def _(part=part):
                for p, dy, dz, share, *moves in part:
                    sign = 1 - 2 * ((me.z + dz) % 2)
                    z = (me.z - sign * dz + NZ) % NZ
                    y = (me.y - sign * dy + NY) % NY
                    panel = z * NS + y // 2
                    ref = self.piece(p, panel)
                    wait(ref, self.recv.at[p * HALF + panel])
                    for move in moves:
                        self.send(p, panel, sign, move)
                    if share:
                        start(ref, ref, self.sent, self.pair, at(me.x, me.y, me.z, 1 - me.k))

    def finish(self):
        me = self.me

        @pl.when(me.source)
        def _():
            wait(self.pan.at[pl.ds(0, HALF - 1)], self.pair)

        @pl.when(me.on_row & jnp.logical_not(me.source))
        def _():
            wait(self.pan.at[pl.ds(0, HALF + 1)], self.pair)

        @pl.when(jnp.logical_not(me.on_row))
        def _():
            wait(self.pan.at[pl.ds(0, HALF)], self.pair)

    def end(self):
        me = self.me
        count = jnp.where(me.source, sum(move[2] for moves in ROOT for move in moves) + 2 * PARTS, 0)
        for (core, on_row), steps in STEPS.items():
            total = sum(step[3] + sum(move[2] for move in step[4:]) for step in steps)
            count = count + jnp.where((me.k == core) & (me.on_row == on_row), total, 0)
        bulk = HALF * PARTS
        loop(0, count // bulk, lambda i: wait(self.pan.at[pl.ds(0, HALF)], self.sent))
        loop(0, count % bulk, lambda i: wait(self.piece(0, 0), self.sent))


def aggregate(coords, lhs, pan, rhs):
    def pick(i):
        column = coords[0, 0, 1, i]
        slot = (column % 2) * HALF + column // 8
        rhs[pl.ds(pl.multiple_of(i * TILE, TILE), TILE), :] = pan[slot]

    loop(0, KMAX, pick)
    return jnp.dot(lhs[...], rhs[...], preferred_element_type=F32)


def kernel(features, weight_in, cotangent_in, coords_in, tiles_in, act_ref, grad_ref, wg_ref,
           coords, pan1, pan2, weight, cotangent, tiles, lhs, rhs, hx, hid, slope_ref,
           wgp, ws, wt, wy, wz, wall, bp, bx, ig,
           f_sem, w_sem, c_sem, t_sem, i_sem, recv1, recv2, sent1, sent2, pair1, pair2, hx_recv, hx_sent, hid_recv,
           ws_recv, ws_sent, wy_recv, wz_recv, wq_recv, wx_recv, w_sent, wx_sent, bx_recv, ig_recv, b_sent):
    me = Place()
    x, y, z, k = me.x, me.y, me.z, me.k

    own = [
        pltpu.make_async_copy(features.at[pl.ds(half * TILE, TILE)],
                              pan1.at[half * HALF + me.panel], f_sem.at[half])
        for half in range(2)
    ]

    @pl.when(me.source)
    def _():
        own[0].start()
        own[1].start()

    coords_copy = pltpu.make_async_copy(coords_in, coords, i_sem)
    coords_copy.start()
    tiles_copy = pltpu.make_async_copy(tiles_in.at[0, 0], tiles, t_sem)
    tiles_copy.start()
    weight_copy = pltpu.make_async_copy(weight_in, weight, w_sem)
    weight_copy.start()
    cotangent_copy = pltpu.make_async_copy(cotangent_in, cotangent, c_sem)
    cotangent_copy.start()

    barrier = pltpu.get_barrier_semaphore()

    def hello(d):
        for core in range(2):
            pl.semaphore_signal(barrier, inc=1, device_id=at(x, (y + d) % NY, z, core),
                                device_id_type=MESH)
            pl.semaphore_signal(barrier, inc=1, device_id=at(x, y, (z + d) % NZ, core),
                                device_id_type=MESH)

    loop(1, NY, hello)
    for d in range(1, NX):
        pl.semaphore_signal(barrier, inc=1, device_id=at((x + d) % NX, y, z, k),
                            device_id_type=MESH)
    pl.semaphore_signal(barrier, inc=1, device_id=at(x, y, z, 1 - k), device_id_type=MESH)

    @pl.when(me.source)
    def _():
        own[0].wait()
        own[1].wait()

    pl.semaphore_wait(barrier, 4 * (NY - 1) + NX)

    one = Gather(me, pan1, recv1, sent1, pair1)
    two = Gather(me, pan2, recv2, sent2, pair2)

    @pl.when(me.source)
    def _():
        one.root(range(2 * PARTS))
        one.mate()

    coords_copy.wait()
    tiles_copy.wait()

    def lay(i):
        row = coords[0, 0, 0, i]
        tile = tiles[i]
        columns = pl.ds(pl.multiple_of(i * TILE, TILE), TILE)
        zero = jnp.zeros_like(tile)
        lhs[0:TILE, columns] = jnp.where(row == 0, tile, zero)
        lhs[TILE:, columns] = jnp.where(row == 0, zero, tile)

    loop(0, KMAX, lay)
    weight_copy.wait()
    cotangent_copy.wait()

    one.forward(0, 1)
    one.finish()
    partial = aggregate(coords, lhs, pan1, rhs)

    home = 2 * (y % 2) + k
    halves = [pl.ds(half * TILE, TILE) for half in range(2)]
    for half, rows in enumerate(halves):
        hx[x, rows, :] = partial[half * TILE:(half + 1) * TILE, :].astype(BF)

        @pl.when(home != x)
        def _(half=half, rows=rows):
            start(hx.at[x, rows], hx.at[x, rows], hx_sent, hx_recv.at[half * NX + x],
                  at(home, y, z, k))

    def middle(rows):
        v = jnp.dot(hid[rows, :], weight[...], preferred_element_type=F32)
        s = 1.0 / (1.0 + jnp.exp(-v))
        slope = cotangent[rows, :].astype(F32) * (s * (1.0 + v * (1.0 - s)))
        slope_ref[rows, :] = slope.astype(BF)
        act_ref[rows, :] = (v * s).astype(BF)

    @pl.when(me.source)
    def _():
        for half, rows in enumerate(halves):
            def take(d, half=half, rows=rows):
                other = (x + d) % NX
                wait(hx.at[other, rows], hx_recv.at[half * NX + other])

            loop(1, NX, take)
            terms = [hx[j, rows, :].astype(F32) for j in range(NX)]
            hid[rows, :] = ((terms[0] + terms[1]) + (terms[2] + terms[3])).astype(BF)
            middle(rows)
            pan2[half * HALF + me.panel] = slope_ref[rows, :]
            two.root(range(half, 2 * PARTS, 2))
        two.mate()

        def tell(d):
            start(hid, hid, hx_sent, hid_recv, at((x + d) % NX, y, z, k))

        for d in (2, 1, 3):
            tell(d)

    two.forward(0, CUTS[0])

    @pl.when(jnp.logical_not(me.source))
    def _():
        wait(hid, hid_recv)
        for rows in halves:
            middle(rows)

    def begin_term():
        term = lax.dot_general(hid[...], slope_ref[...], (((0,), (0,)), ((), ())),
                               preferred_element_type=F32)
        wgp[0] = term[:, 0:TILE]
        wgp[1] = term[:, TILE:]
        start(wgp.at[1 - k, rows64], ws, ws_sent, ws_recv.at[0], at(x, y, z, 1 - k))

    rows64 = pl.ds(pl.multiple_of(x * 64, 64), 64)
    begin_term()

    two.forward(CUTS[0], CUTS[1])

    wait(ws, ws_recv.at[0])
    wt[...] = (wgp[k, rows64, :] + ws[...]).reshape(NY, 8, TILE)

    def scatter_y(d):
        to = (y + d) % NY
        start(wt.at[to], wy.at[y], w_sent, wy_recv.at[y], at(x, to, z, k))

    loop(1, NY, scatter_y)
    wy[y] = wt[y]

    two.forward(CUTS[1], CUTS[2])

    def take_y(d):
        src = (y + d) % NY
        wait(wy.at[src], wy_recv.at[src])

    loop(1, NY, take_y)
    wz[z] = jnp.sum(wy[...], axis=0)

    def scatter_z(d):
        start(wz.at[z], wz.at[z], w_sent, wz_recv.at[z], at(x, y, (z + d) % NZ, k))

    loop(1, NZ, scatter_z)

    two.forward(CUTS[2], CUTS[3])

    def take_z(d):
        src = (z + d) % NZ
        wait(wz.at[src], wz_recv.at[src])

    loop(1, NZ, take_z)
    wall[k, x, y] = jnp.sum(wz[...], axis=0) * (1.0 / math.sqrt(ROWS * NY * NZ * 2))

    def spread_y(d):
        start(wall.at[k, x, y], wall.at[k, x, y], w_sent, wq_recv.at[y], at(x, (y + d) % NY, z, k))

    loop(1, NY, spread_y)

    two.forward(CUTS[3], 1)
    two.finish()

    bp[...] = aggregate(coords, lhs, pan2, rhs).astype(BF).reshape(NX, 64, F)

    def give_back(d):
        to = (x + d) % NX
        start(bp.at[to], bx.at[x], b_sent, bx_recv.at[x], at(to, y, z, k))

    for d in (2, 1, 3):
        give_back(d)
    bx[x] = bp[x]

    def take_q(d):
        src = (y + d) % NY
        wait(wall.at[k, x, src], wq_recv.at[src])

    loop(1, NY, take_q)

    def spread_x(d):
        start(wall.at[k, x], wall.at[k, x], wx_sent, wx_recv.at[x], at((x + d) % NX, y, z, k))

    for d in (2, 1, 3):
        spread_x(d)

    def take_back(d):
        wait(bx.at[(x + d) % NX], bx_recv.at[(x + d) % NX])

    loop(1, NX, take_back)
    total = (bx[0].astype(F32) + bx[1].astype(F32)) + (bx[2].astype(F32) + bx[3].astype(F32))
    ig[x] = lax.dot_general(total.astype(BF), weight[...], (((1,), (1,)), ((), ())),
                            preferred_element_type=F32).astype(BF)

    def give_grad(d):
        start(ig.at[x], ig.at[x], b_sent, ig_recv.at[x], at((x + d) % NX, y, z, k))

    for d in (2, 1, 3):
        give_grad(d)

    def take_x(d):
        wait(wall.at[k, (x + d) % NX], wx_recv.at[(x + d) % NX])

    loop(1, NX, take_x)
    start(wall.at[k], wall.at[k], ws_sent, ws_recv.at[1], at(x, y, z, 1 - k))

    one.end()
    two.end()
    loop(0, jnp.where(me.source, NX - 1, 1), lambda d: wait(hx.at[0], hx_sent))
    loop(0, 7 + 7 + 7, lambda i: wait(wz.at[0], w_sent))

    def take_grad(d):
        wait(ig.at[(x + d) % NX], ig_recv.at[(x + d) % NX])

    loop(1, NX, take_grad)
    grad_ref[...] = ig[...].reshape(ROWS, F)
    wait(wall.at[1 - k], ws_recv.at[1])
    for half in range(2):
        for quarter in range(NX):
            wg_ref[quarter * 64:quarter * 64 + 64, half * TILE:(half + 1) * TILE] = (
                wall[half, quarter].reshape(64, TILE))
    loop(1, NX, lambda d: wait(wall.at[0, 0], wx_sent))
    wait(ws, ws_sent)
    wait(wall.at[0], ws_sent)
    loop(0, 6, lambda i: wait(bp.at[0], b_sent))


CUTS = (0.2, 0.3, 0.55, 0.85)


def write_out(act, grad, wg, act_out, grad_out, wg_out, sems):
    copies = [
        pltpu.make_async_copy(src, dst, sems.at[i])
        for i, (src, dst) in enumerate(((act, act_out), (grad, grad_out), (wg, wg_out)))
    ]
    for copy in copies:
        copy.start()
    for copy in copies:
        copy.wait()


def pin(value):
    return pltpu.with_memory_space_constraint(value, pltpu.HBM)


def on_device(features, weight, cotangent, tile_coords, tile_count, tiles):
    vmem = pl.BlockSpec(memory_space=pltpu.VMEM)
    hbm = pl.BlockSpec(memory_space=pltpu.HBM)
    dma = pltpu.SemaphoreType.DMA
    shapes = (
        jax.ShapeDtypeStruct((ROWS, F), BF),
        jax.ShapeDtypeStruct((ROWS, F), BF),
        jax.ShapeDtypeStruct((F, F), F32),
    )
    results = pl.pallas_call(
        kernel,
        out_shape=(pltpu.VMEM((ROWS, F), BF), pltpu.VMEM((ROWS, F), BF), pltpu.VMEM((F, F), F32)),
        in_specs=[hbm, hbm, hbm, hbm, hbm],
        out_specs=(vmem, vmem, vmem),
        scratch_shapes=[
            pltpu.SMEM((1, 1, 2, KMAX), jnp.int32),
            pltpu.VMEM((2 * HALF, TILE, F), BF),
            pltpu.VMEM((2 * HALF, TILE, F), BF),
            pltpu.VMEM((F, F), BF),
            pltpu.VMEM((ROWS, F), BF),
            pltpu.VMEM((KMAX, TILE, TILE), BF),
            pltpu.VMEM((2 * TILE, KMAX * TILE), BF),
            pltpu.VMEM((KMAX * TILE, F), BF),
            pltpu.VMEM((NX, ROWS, F), BF),
            pltpu.VMEM((ROWS, F), BF),
            pltpu.VMEM((ROWS, F), BF),
            pltpu.VMEM((2, F, TILE), F32),
            pltpu.VMEM((64, TILE), F32),
            pltpu.VMEM((NY, 8, TILE), F32),
            pltpu.VMEM((NY, 8, TILE), F32),
            pltpu.VMEM((NZ, 8, TILE), F32),
            pltpu.VMEM((2, NX, NY, 8, TILE), F32),
            pltpu.VMEM((NX, 64, F), BF),
            pltpu.VMEM((NX, 64, F), BF),
            pltpu.VMEM((NX, 64, F), BF),
            dma((2,)), dma(()), dma(()), dma(()), dma(()),
            dma((2 * PARTS * HALF,)), dma((2 * PARTS * HALF,)), dma(()), dma(()), dma(()), dma(()),
            dma((2 * NX,)), dma(()), dma(()),
            dma((2,)), dma(()), dma((NY,)), dma((NZ,)), dma((NY,)), dma((NX,)), dma(()), dma(()),
            dma((NX,)), dma((NX,)), dma(()),
        ],
        compiler_params=pltpu.CompilerParams(
            collective_id=0, has_side_effects=True, vmem_limit_bytes=24 << 20
        ),
        name="graph_layer",
    )(pin(features), pin(weight), pin(cotangent), pin(jnp.swapaxes(tile_coords, 2, 3)), pin(tiles))
    return pl.pallas_call(
        write_out,
        out_shape=shapes,
        in_specs=[vmem, vmem, vmem],
        out_specs=(hbm, hbm, hbm),
        scratch_shapes=[dma((3,))],
        compiler_params=pltpu.CompilerParams(vmem_limit_bytes=4 << 20),
        name="write_out",
    )(*[pltpu.with_memory_space_constraint(result, pltpu.VMEM) for result in results])


def solution(mesh):
    placed = (
        P("rows", None),
        P(),
        P("rows", None),
        P("rows", "rep", None, None),
        P("rows", "rep"),
        P("rows", "rep", None, None, None),
    )
    return jax.shard_map(
        on_device,
        mesh=mesh,
        in_specs=placed,
        out_specs=(P("rows", None), P("rows", None), P()),
        check_vma=False,
    )
```

```python
import math

import jax
import jax.numpy as jnp
from jax import lax
from jax.experimental import pallas as pl
from jax.experimental.pallas import tpu as pltpu
from jax.sharding import PartitionSpec as P

MESH = pl.DeviceIdType.MESH
NX, NY, NZ = 4, 8, 8
NS = NY // 2
HALF = NS * NZ
ROWS, F, TILE, KMAX = 256, 256, 128, 20
BF, F32 = jnp.bfloat16, jnp.float32

PARTS = 1
ROOT = (
    ((-1,0,1), (0,1,1), (0,-3,1), (2,0,1), (1,0,1),),
    ((0,1,1), (3,0,1), (0,-2,1), (-1,0,1), (-2,0,1), (0,-1,1), (0,2,1), (1,0,1),),
)
STEPS = {
    (0, True): (
        (0,0,1,1,(-2,0,1),(0,1,1)), (0,2,0,1,(0,3,1),(0,1,1),(1,0,1),(0,-1,1)),
        (0,0,-3,1,(1,0,1),(0,1,1),(0,-1,1)), (0,-2,0,1), (0,-2,1,1,(-1,0,1),(0,1,1)),
        (0,0,2,1,(-1,0,1),(0,1,1)), (0,2,1,1,(1,0,1)), (0,2,3,1,(0,-1,1),(1,0,1),(-1,0,1)),
        (0,2,-1,1,(0,-1,1)), (0,-2,-1,1), (0,0,4,1,(-1,0,1)), (0,0,-2,1,(1,0,1)), (0,0,-1,1),
        (0,4,0,1,(0,-3,1)), (0,0,3,1), (0,-2,2,1,(0,1,1)), (0,-2,-3,1), (0,-2,-2,1), (0,2,2,1,(-1,0,1)),
        (0,2,-3,1,(0,-1,1),(1,0,1)), (0,2,-2,1), (0,4,1,1,(0,1,1)), (0,4,-1,1), (0,-2,3,1,(0,1,1)), (0,4,3,1),
        (0,4,-3,1), (0,2,4,1), (0,4,2,1), (0,4,-2,1), (0,4,4,1), (0,-2,4,1),
    ),
    (0, False): (
        (0,-1,0,1,(-2,0,1),(0,-1,1),(0,-3,1),(0,3,1),(-1,0,1),(0,1,1)), (0,1,0,1,(0,-1,1),(0,1,1)),
        (0,-1,-1,1,(0,-1,1),(-1,0,1),(1,0,1)), (0,-1,1,1), (0,-3,0,1,(0,3,1),(0,-1,1),(-1,0,1)), (0,-1,3,1),
        (0,-1,-3,1,(-1,0,1)), (0,3,0,1,(0,-1,1)), (0,1,1,1), (0,1,-1,1), (0,-1,-2,1,(-1,0,1)),
        (0,1,-3,1,(0,-1,1),(1,0,1)), (0,-3,1,1,(-1,0,1)), (0,-3,-1,1,(0,-1,1),(-1,0,1)), (0,-1,2,1),
        (0,-3,3,1,(0,1,1),(0,-1,1),(-1,0,1)), (0,3,-1,1,(0,-1,1)), (0,3,1,1,(0,1,1)), (0,3,3,1,(0,1,1)),
        (0,1,3,1), (0,1,4,1,(3,0,1)), (0,-1,4,1), (0,-3,-2,1,(-1,0,1)), (0,1,-2,1), (0,-3,4,1,(0,1,1)),
        (0,-3,2,1), (0,3,-2,1), (0,3,2,1), (0,1,2,1), (0,3,4,1), (0,3,-3,1), (0,-3,-3,1),
    ),
    (1, True): (
        (1,0,1,1,(0,2,1),(1,0,1),(3,0,1),(-1,0,1)), (1,0,-2,1,(0,-1,1),(2,0,1),(-1,0,1),(1,0,1)),
        (1,0,-1,1,(-1,0,1),(1,0,1)), (1,-2,0,1,(0,1,1),(0,-2,1),(0,-1,1)),
        (1,0,3,1,(0,1,1),(1,0,1),(-2,0,1),(-1,0,1)), (1,0,2,1), (1,0,-3,1,(1,0,1),(-2,0,1),(-1,0,1)),
        (1,4,0,1,(0,2,1)), (1,2,0,1), (1,2,-2,1,(0,-2,1),(0,-1,1)), (1,2,1,1,(0,1,1)), (1,-2,1,1,(-1,0,1)),
        (1,-2,-2,1), (1,-2,-1,1), (1,2,-1,1), (1,0,4,1,(-3,0,1),(1,0,1)), (1,4,1,1,(0,2,1)),
        (1,-2,3,1,(-1,0,1),(0,1,1)), (1,-2,-3,1,(-1,0,1)), (1,4,2,1), (1,2,-3,1), (1,-2,2,1),
        (1,2,4,1,(1,0,1)), (1,2,2,1,(1,0,1)), (1,2,3,1,(1,0,1)), (1,4,-2,1,(0,1,1)), (1,-2,4,1), (1,4,3,1),
        (1,4,-3,1), (1,4,-1,1), (1,4,4,1),
    ),
    (1, False): (
        (1,-1,0,1,(-2,0,1)), (1,3,0,1,(0,-1,1),(1,0,1),(-1,0,1)), (1,1,0,1), (1,1,1,1,(1,0,1),(0,1,1)),
        (1,-1,1,1,(0,1,1)), (1,3,-1,1,(0,-1,1),(-1,0,1)), (1,3,1,1,(1,0,1)), (1,-1,-2,1,(0,-2,1)),
        (1,-3,0,1,(0,-1,1),(0,2,1)), (1,1,-2,1), (1,1,2,1), (1,-1,-1,1), (1,-1,2,1,(-1,0,1)), (1,1,-1,1),
        (1,1,3,1,(1,0,1)), (1,3,-2,1,(1,0,1),(0,-1,1)), (1,-1,3,1), (1,1,-3,1,(3,0,1)), (1,-1,-3,1),
        (1,-1,4,1), (1,-3,-1,1,(0,-1,1)), (1,-3,2,1), (1,-3,1,1), (1,3,-3,1), (1,1,4,1), (1,-3,4,1,(-1,0,1)),
        (1,-3,3,1), (1,-3,-3,1), (1,-3,-2,1), (1,3,2,1), (1,3,3,1), (1,3,4,1),
    ),
}
PIECE = TILE // PARTS


def at(x, y, z, k):
    return ((z * NY + y) * 2 + k, x)


def start(src, dst, send_sem, recv_sem, device):
    pltpu.make_async_remote_copy(
        src_ref=src, dst_ref=dst, send_sem=send_sem, recv_sem=recv_sem,
        device_id=device, device_id_type=MESH,
    ).start()


def wait(ref, sem):
    pltpu.make_async_copy(ref, ref, sem).wait()


def loop(low, high, body):
    def step(index, carry):
        body(index)
        return carry

    lax.fori_loop(low, high, step, 0)


class Place:
    def __init__(self):
        rows = lax.axis_index("rows")
        self.x = lax.axis_index("rep")
        self.k = rows % 2
        self.y = (rows // 2) % NY
        self.z = rows // (2 * NY)
        self.owner = self.x % 2
        self.on_row = self.y % 2 == self.x // 2
        self.source = self.on_row & (self.k == self.owner)
        self.panel = self.z * NS + self.y // 2


class Gather:
    def __init__(self, me, pan, recv, sent, pair):
        self.me, self.pan, self.recv, self.sent, self.pair = me, pan, recv, sent, pair

    def piece(self, p, panel):
        return self.pan.at[(p % 2) * HALF + panel, pl.ds((p // 2) * PIECE, PIECE)]

    def send(self, p, panel, sign, move):
        dy, dz, cores = move
        ref = self.piece(p, panel)
        y = (self.me.y + sign * dy + NY) % NY
        z = (self.me.z + sign * dz + NZ) % NZ
        start(ref, ref, self.sent, self.recv.at[p * HALF + panel], at(self.me.x, y, z, p % 2))
        if cores == 2:
            start(ref, ref, self.sent, self.pair, at(self.me.x, y, z, 1 - p % 2))

    def root(self, pieces):
        sign = 1 - 2 * (self.me.z % 2)
        for turn in range(max(len(ROOT[p]) for p in pieces)):
            for p in pieces:
                if turn < len(ROOT[p]):
                    self.send(p, self.me.panel, sign, ROOT[p][turn])

    def mate(self):
        me = self.me
        for half in range(2):
            ref = self.pan.at[half * HALF + me.panel]
            start(ref, ref, self.sent, self.pair, at(me.x, me.y, me.z, 1 - me.k))

    def forward(self, low, high):
        me = self.me
        for (core, on_row), steps in STEPS.items():
            part = steps[round(low * len(steps)):round(high * len(steps))]

            @pl.when((me.k == core) & (me.on_row == on_row))
            def _(part=part):
                for p, dy, dz, share, *moves in part:
                    sign = 1 - 2 * ((me.z + dz) % 2)
                    z = (me.z - sign * dz + NZ) % NZ
                    y = (me.y - sign * dy + NY) % NY
                    panel = z * NS + y // 2
                    ref = self.piece(p, panel)
                    wait(ref, self.recv.at[p * HALF + panel])
                    for move in moves:
                        self.send(p, panel, sign, move)
                    if share:
                        start(ref, ref, self.sent, self.pair, at(me.x, me.y, me.z, 1 - me.k))

    def finish(self):
        me = self.me

        @pl.when(me.source)
        def _():
            wait(self.pan.at[pl.ds(0, HALF - 1)], self.pair)

        @pl.when(me.on_row & jnp.logical_not(me.source))
        def _():
            wait(self.pan.at[pl.ds(0, HALF + 1)], self.pair)

        @pl.when(jnp.logical_not(me.on_row))
        def _():
            wait(self.pan.at[pl.ds(0, HALF)], self.pair)

    def end(self):
        me = self.me
        count = jnp.where(me.source, sum(move[2] for moves in ROOT for move in moves) + 2 * PARTS, 0)
        for (core, on_row), steps in STEPS.items():
            total = sum(step[3] + sum(move[2] for move in step[4:]) for step in steps)
            count = count + jnp.where((me.k == core) & (me.on_row == on_row), total, 0)
        bulk = HALF * PARTS
        loop(0, count // bulk, lambda i: wait(self.pan.at[pl.ds(0, HALF)], self.sent))
        loop(0, count % bulk, lambda i: wait(self.piece(0, 0), self.sent))


def aggregate(coords, lhs, pan, rhs):
    def pick(i):
        column = coords[0, 0, 1, i]
        slot = (column % 2) * HALF + column // 8
        rhs[pl.ds(pl.multiple_of(i * TILE, TILE), TILE), :] = pan[slot]

    loop(0, KMAX, pick)
    return jnp.dot(lhs[...], rhs[...], preferred_element_type=F32)


def kernel(features, weight_in, cotangent_in, coords_in, tiles_in, act_ref, grad_ref, wg_ref,
           coords, pan1, pan2, weight, cotangent, tiles, lhs, rhs, hx, hid, slope_ref,
           wgp, ws, wt, wy, wz, wall, bp, bx, ig,
           f_sem, w_sem, c_sem, t_sem, i_sem, recv1, recv2, sent1, sent2, pair1, pair2, hx_recv, hx_sent, hid_recv,
           ws_recv, ws_sent, wy_recv, wz_recv, wq_recv, wx_recv, w_sent, wx_sent, bx_recv, ig_recv, b_sent):
    me = Place()
    x, y, z, k = me.x, me.y, me.z, me.k

    own = [
        pltpu.make_async_copy(features.at[pl.ds(half * TILE, TILE)],
                              pan1.at[half * HALF + me.panel], f_sem.at[half])
        for half in range(2)
    ]

    @pl.when(me.source)
    def _():
        own[0].start()
        own[1].start()

    coords_copy = pltpu.make_async_copy(coords_in, coords, i_sem)
    coords_copy.start()
    tiles_copy = pltpu.make_async_copy(tiles_in.at[0, 0], tiles, t_sem)
    tiles_copy.start()
    weight_copy = pltpu.make_async_copy(weight_in, weight, w_sem)
    weight_copy.start()
    cotangent_copy = pltpu.make_async_copy(cotangent_in, cotangent, c_sem)
    cotangent_copy.start()

    barrier = pltpu.get_barrier_semaphore()

    def hello(d):
        for core in range(2):
            pl.semaphore_signal(barrier, inc=1, device_id=at(x, (y + d) % NY, z, core),
                                device_id_type=MESH)
            pl.semaphore_signal(barrier, inc=1, device_id=at(x, y, (z + d) % NZ, core),
                                device_id_type=MESH)

    loop(1, NY, hello)
    for d in range(1, NX):
        pl.semaphore_signal(barrier, inc=1, device_id=at((x + d) % NX, y, z, k),
                            device_id_type=MESH)
    pl.semaphore_signal(barrier, inc=1, device_id=at(x, y, z, 1 - k), device_id_type=MESH)

    @pl.when(me.source)
    def _():
        own[0].wait()
        own[1].wait()

    pl.semaphore_wait(barrier, 4 * (NY - 1) + NX)

    one = Gather(me, pan1, recv1, sent1, pair1)
    two = Gather(me, pan2, recv2, sent2, pair2)

    @pl.when(me.source)
    def _():
        one.root(range(2 * PARTS))
        one.mate()

    coords_copy.wait()
    tiles_copy.wait()

    def lay(i):
        row = coords[0, 0, 0, i]
        tile = tiles[i]
        columns = pl.ds(pl.multiple_of(i * TILE, TILE), TILE)
        zero = jnp.zeros_like(tile)
        lhs[0:TILE, columns] = jnp.where(row == 0, tile, zero)
        lhs[TILE:, columns] = jnp.where(row == 0, zero, tile)

    loop(0, KMAX, lay)
    weight_copy.wait()
    cotangent_copy.wait()

    one.forward(0, 1)
    one.finish()
    partial = aggregate(coords, lhs, pan1, rhs)

    home = 2 * (y % 2) + k
    halves = [pl.ds(half * TILE, TILE) for half in range(2)]
    for half, rows in enumerate(halves):
        hx[x, rows, :] = partial[half * TILE:(half + 1) * TILE, :].astype(BF)

        @pl.when(home != x)
        def _(half=half, rows=rows):
            start(hx.at[x, rows], hx.at[x, rows], hx_sent, hx_recv.at[half * NX + x],
                  at(home, y, z, k))

    def middle(rows):
        v = jnp.dot(hid[rows, :], weight[...], preferred_element_type=F32)
        s = 1.0 / (1.0 + jnp.exp(-v))
        slope = cotangent[rows, :].astype(F32) * (s * (1.0 + v * (1.0 - s)))
        slope_ref[rows, :] = slope.astype(BF)
        act_ref[rows, :] = (v * s).astype(BF)

    def begin_term():
        term = lax.dot_general(hid[...], slope_ref[...], (((0,), (0,)), ((), ())),
                               preferred_element_type=F32)
        wgp[0] = term[:, 0:TILE]
        wgp[1] = term[:, TILE:]
        start(wgp.at[1 - k, rows64], ws, ws_sent, ws_recv.at[0], at(x, y, z, 1 - k))

    rows64 = pl.ds(pl.multiple_of(x * 64, 64), 64)
    @pl.when(me.source)
    def _():
        for half, rows in enumerate(halves):
            def take(d, half=half, rows=rows):
                other = (x + d) % NX
                wait(hx.at[other, rows], hx_recv.at[half * NX + other])

            loop(1, NX, take)
            terms = [hx[j, rows, :].astype(F32) for j in range(NX)]
            hid[rows, :] = ((terms[0] + terms[1]) + (terms[2] + terms[3])).astype(BF)
            middle(rows)
            pan2[half * HALF + me.panel] = slope_ref[rows, :]
            two.root(range(half, 2 * PARTS, 2))
        def tell(d):
            start(hid, hid, hx_sent, hid_recv, at((x + d) % NX, y, z, k))

        for d in (2, 1, 3):
            tell(d)
        two.mate()
        begin_term()

    two.forward(0, CUTS[0])

    @pl.when(jnp.logical_not(me.source))
    def _():
        wait(hid, hid_recv)
        for rows in halves:
            middle(rows)
        begin_term()


    two.forward(CUTS[0], CUTS[1])

    wait(ws, ws_recv.at[0])
    wt[...] = (wgp[k, rows64, :] + ws[...]).reshape(NY, 8, TILE)

    def scatter_y(d):
        to = (y + d) % NY
        start(wt.at[to], wy.at[y], w_sent, wy_recv.at[y], at(x, to, z, k))

    loop(1, NY, scatter_y)
    wy[y] = wt[y]

    two.forward(CUTS[1], CUTS[2])

    def take_y(d):
        src = (y + d) % NY
        wait(wy.at[src], wy_recv.at[src])

    loop(1, NY, take_y)
    wz[z] = jnp.sum(wy[...], axis=0)

    def scatter_z(d):
        start(wz.at[z], wz.at[z], w_sent, wz_recv.at[z], at(x, y, (z + d) % NZ, k))

    loop(1, NZ, scatter_z)

    two.forward(CUTS[2], CUTS[3])

    def take_z(d):
        src = (z + d) % NZ
        wait(wz.at[src], wz_recv.at[src])

    loop(1, NZ, take_z)
    wall[k, x, y] = jnp.sum(wz[...], axis=0) * (1.0 / math.sqrt(ROWS * NY * NZ * 2))

    def spread_y(d):
        start(wall.at[k, x, y], wall.at[k, x, y], w_sent, wq_recv.at[y], at(x, (y + d) % NY, z, k))

    loop(1, NY, spread_y)

    two.forward(CUTS[3], 1)
    two.finish()

    bp[...] = aggregate(coords, lhs, pan2, rhs).astype(BF).reshape(NX, 64, F)

    def give_back(d):
        to = (x + d) % NX
        start(bp.at[to], bx.at[x], b_sent, bx_recv.at[x], at(to, y, z, k))

    for d in (2, 1, 3):
        give_back(d)
    bx[x] = bp[x]

    def take_q(d):
        src = (y + d) % NY
        wait(wall.at[k, x, src], wq_recv.at[src])

    loop(1, NY, take_q)

    def spread_x(d):
        start(wall.at[k, x], wall.at[k, x], wx_sent, wx_recv.at[x], at((x + d) % NX, y, z, k))

    for d in (2, 1, 3):
        spread_x(d)

    def take_back(d):
        wait(bx.at[(x + d) % NX], bx_recv.at[(x + d) % NX])

    loop(1, NX, take_back)
    total = (bx[0].astype(F32) + bx[1].astype(F32)) + (bx[2].astype(F32) + bx[3].astype(F32))
    ig[x] = lax.dot_general(total.astype(BF), weight[...], (((1,), (1,)), ((), ())),
                            preferred_element_type=F32).astype(BF)

    def give_grad(d):
        start(ig.at[x], ig.at[x], b_sent, ig_recv.at[x], at((x + d) % NX, y, z, k))

    for d in (2, 1, 3):
        give_grad(d)

    def take_x(d):
        wait(wall.at[k, (x + d) % NX], wx_recv.at[(x + d) % NX])

    loop(1, NX, take_x)
    start(wall.at[k], wall.at[k], ws_sent, ws_recv.at[1], at(x, y, z, 1 - k))

    one.end()
    two.end()
    loop(0, jnp.where(me.source, NX - 1, 1), lambda d: wait(hx.at[0], hx_sent))
    loop(0, 7 + 7 + 7, lambda i: wait(wz.at[0], w_sent))

    def take_grad(d):
        wait(ig.at[(x + d) % NX], ig_recv.at[(x + d) % NX])

    loop(1, NX, take_grad)
    grad_ref[...] = ig[...].reshape(ROWS, F)
    wait(wall.at[1 - k], ws_recv.at[1])
    for half in range(2):
        for quarter in range(NX):
            wg_ref[quarter * 64:quarter * 64 + 64, half * TILE:(half + 1) * TILE] = (
                wall[half, quarter].reshape(64, TILE))
    loop(1, NX, lambda d: wait(wall.at[0, 0], wx_sent))
    wait(ws, ws_sent)
    wait(wall.at[0], ws_sent)
    loop(0, 6, lambda i: wait(bp.at[0], b_sent))


CUTS = (0.2, 0.3, 0.55, 0.85)


def write_out(act, grad, wg, act_out, grad_out, wg_out, sems):
    copies = [
        pltpu.make_async_copy(src, dst, sems.at[i])
        for i, (src, dst) in enumerate(((act, act_out), (grad, grad_out), (wg, wg_out)))
    ]
    for copy in copies:
        copy.start()
    for copy in copies:
        copy.wait()


def pin(value):
    return pltpu.with_memory_space_constraint(value, pltpu.HBM)


def on_device(features, weight, cotangent, tile_coords, tile_count, tiles):
    vmem = pl.BlockSpec(memory_space=pltpu.VMEM)
    hbm = pl.BlockSpec(memory_space=pltpu.HBM)
    dma = pltpu.SemaphoreType.DMA
    shapes = (
        jax.ShapeDtypeStruct((ROWS, F), BF),
        jax.ShapeDtypeStruct((ROWS, F), BF),
        jax.ShapeDtypeStruct((F, F), F32),
    )
    results = pl.pallas_call(
        kernel,
        out_shape=(pltpu.VMEM((ROWS, F), BF), pltpu.VMEM((ROWS, F), BF), pltpu.VMEM((F, F), F32)),
        in_specs=[hbm, hbm, hbm, hbm, hbm],
        out_specs=(vmem, vmem, vmem),
        scratch_shapes=[
            pltpu.SMEM((1, 1, 2, KMAX), jnp.int32),
            pltpu.VMEM((2 * HALF, TILE, F), BF),
            pltpu.VMEM((2 * HALF, TILE, F), BF),
            pltpu.VMEM((F, F), BF),
            pltpu.VMEM((ROWS, F), BF),
            pltpu.VMEM((KMAX, TILE, TILE), BF),
            pltpu.VMEM((2 * TILE, KMAX * TILE), BF),
            pltpu.VMEM((KMAX * TILE, F), BF),
            pltpu.VMEM((NX, ROWS, F), BF),
            pltpu.VMEM((ROWS, F), BF),
            pltpu.VMEM((ROWS, F), BF),
            pltpu.VMEM((2, F, TILE), F32),
            pltpu.VMEM((64, TILE), F32),
            pltpu.VMEM((NY, 8, TILE), F32),
            pltpu.VMEM((NY, 8, TILE), F32),
            pltpu.VMEM((NZ, 8, TILE), F32),
            pltpu.VMEM((2, NX, NY, 8, TILE), F32),
            pltpu.VMEM((NX, 64, F), BF),
            pltpu.VMEM((NX, 64, F), BF),
            pltpu.VMEM((NX, 64, F), BF),
            dma((2,)), dma(()), dma(()), dma(()), dma(()),
            dma((2 * PARTS * HALF,)), dma((2 * PARTS * HALF,)), dma(()), dma(()), dma(()), dma(()),
            dma((2 * NX,)), dma(()), dma(()),
            dma((2,)), dma(()), dma((NY,)), dma((NZ,)), dma((NY,)), dma((NX,)), dma(()), dma(()),
            dma((NX,)), dma((NX,)), dma(()),
        ],
        compiler_params=pltpu.CompilerParams(
            collective_id=0, has_side_effects=True, vmem_limit_bytes=24 << 20
        ),
        name="graph_layer",
    )(pin(features), pin(weight), pin(cotangent), pin(jnp.swapaxes(tile_coords, 2, 3)), pin(tiles))
    return pl.pallas_call(
        write_out,
        out_shape=shapes,
        in_specs=[vmem, vmem, vmem],
        out_specs=(hbm, hbm, hbm),
        scratch_shapes=[dma((3,))],
        compiler_params=pltpu.CompilerParams(vmem_limit_bytes=4 << 20),
        name="write_out",
    )(*[pltpu.with_memory_space_constraint(result, pltpu.VMEM) for result in results])


def solution(mesh):
    placed = (
        P("rows", None),
        P(),
        P("rows", None),
        P("rows", "rep", None, None),
        P("rows", "rep"),
        P("rows", "rep", None, None, None),
    )
    return jax.shard_map(
        on_device,
        mesh=mesh,
        in_specs=placed,
        out_specs=(P("rows", None), P("rows", None), P()),
        check_vma=False,
    )
```
